32 devices in a mesh: dp: 4 (over y, core), ctx: 8 (over z, x).
Axes of the slice: x: 2, y: 2, z: 4, core: 2. Of those that a mesh axis runs over, the one named last changes fastest.
Arguments:
- query_act: bfloat16 [4096, 4096], P(('dp', 'ctx')), may hold values from -6 to 6
- key_act: bfloat16 [4096, 4096], P(('dp', 'ctx')), may hold values from -6 to 6
- value_act: bfloat16 [4096, 4096], P(('dp', 'ctx')), may hold values from -6 to 6
- out_grad: bfloat16 [4096, 4096], P(('dp', 'ctx')), may hold values from -6 to 6
- filter_taps: float32 [4096, 128], P('ctx'), may hold values from -0.5 to 0.5
- doc_ids: int32 [4096], replicated, may hold values from 0 to 7, as said below
Outputs:
- query_grad: bfloat16 [4096, 4096], P(('dp', 'ctx'))
- key_grad: bfloat16 [4096, 4096], P(('dp', 'ctx'))
- value_grad: bfloat16 [4096, 4096], P(('dp', 'ctx'))
- filter_grad: float32 [4096, 128], P('ctx')
The draws below stay inside these ranges and needn't reach their ends.
Inputs may be any that keep to these rules, and one draw needn't show every extreme that they name: `doc_ids`: the document numbers start at 0, never fall, and rise by one at each boundary; the window holds 8 documents, each of at least 256 positions.
All inputs are finite; a program needn't handle non-finite values.
Results may differ from the reference program's by a relative error of at most 0.0064.
Values may be sent and summed in bfloat16 or wider, within the bound.
No kernel may reach another device: no remote copies, remote signals or barrier semaphores. Data moves between devices by JAX's collectives and lax.ppermute only.
A program may use at most 320 MiB of HBM per device.

```python
import math
import jax
import jax.numpy as jnp
from jax import lax

D = 4096
FL = 128
DOCS = 8
SEQ_LEN = 4096


def draw_doc_ids(key, part):
    spare_rows = SEQ_LEN - DOCS * 2 * FL
    cut_points = jnp.sort(jax.random.randint(key, (DOCS - 1,), 0, spare_rows + 1))
    starts = cut_points + 2 * FL * jnp.arange(1, DOCS, dtype=jnp.int32)
    positions = jnp.arange(SEQ_LEN, dtype=jnp.int32)
    marks = (positions[:, None] >= starts[None, :]).astype(jnp.int32)
    return jnp.sum(marks, axis=1).astype(jnp.int32)


def steps_of(key, extent, split, low, high):
    loudness = 1.0
    for position, blocks in split:
        steps = jax.random.uniform(jax.random.fold_in(jax.random.fold_in(key, 6), position), (blocks,), jnp.float32, low / len(split), high / len(split))
        loudness = loudness * jnp.repeat(jnp.exp(steps), extent[position] // blocks).reshape((-1,) + (1,) * (len(extent) - 1 - position))
    return loudness


def normal_values(rng, dims, scale, reach, split=(), held_as=jnp.bfloat16):
    array = scale * jax.random.normal(rng, dims, jnp.float32)
    if split:
        array = array * steps_of(rng, dims, split, -0.22, 0.18)
    return jnp.clip(array, -reach, reach).astype(held_as)


def setup_inputs(seed: int = 0) -> dict:
    seeds = jax.random.split(jax.random.key(seed), 7)
    query_act = normal_values(seeds[0], (SEQ_LEN, D), 1.0, 6.0, ((0, 32),))
    key_act = normal_values(seeds[1], (SEQ_LEN, D), 1.0, 6.0, ((0, 32),))
    value_act = normal_values(seeds[2], (SEQ_LEN, D), 1.0, 6.0, ((0, 32),))
    out_grad = normal_values(seeds[3], (SEQ_LEN, D), 1.0, 6.0, ((0, 32),))
    filter_taps = normal_values(seeds[4], (D, FL), FL ** -0.5, 0.5, ((0, 8),), jnp.float32)
    doc_ids = draw_doc_ids(jax.random.fold_in(seeds[6], 71), 0)
    return dict(query_act=query_act, key_act=key_act, value_act=value_act, out_grad=out_grad, filter_taps=filter_taps, doc_ids=doc_ids)


def build_toeplitz(tap_rows):
    chan_count, tap_count = tap_rows.shape
    zero_col = jnp.zeros((chan_count, 1), tap_rows.dtype)
    tail_cols = jnp.zeros((chan_count, tap_count), tap_rows.dtype)
    pattern = jnp.concatenate([zero_col, tap_rows[:, ::-1], tail_cols], axis=1)
    tiled = jnp.tile(pattern, (1, tap_count))[:, :tap_count * 2 * tap_count]
    return tiled.reshape(chan_count, tap_count, 2 * tap_count)

def lag_sums(block):
    chan_count, tap_count, span = block.shape
    flat = block.reshape(chan_count, tap_count * span)
    flat = jnp.pad(flat, ((0, 0), (0, tap_count)))
    skewed = flat.reshape(chan_count, tap_count, span + 1)
    summed = lax.optimization_barrier(jnp.sum(skewed[:, :, 1:tap_count + 1], axis=1))
    return summed[:, ::-1]

def mix_exact(kv_ext, g_ext, seg_ext, tap_rows):
    chan_count, tap_count = tap_rows.shape
    block_count = kv_ext.shape[1] // tap_count - 1
    kv_blocks = kv_ext.reshape(chan_count, block_count + 1, tap_count)
    windows = jnp.concatenate([kv_blocks[:, :-1], kv_blocks[:, 1:]], axis=2)
    seg_blocks = seg_ext.reshape(block_count + 2, tap_count)
    seg_win = jnp.concatenate([seg_blocks[:-1], seg_blocks[1:]], axis=1)
    same = (seg_win == seg_win[:, -1:]).astype(jnp.float32)
    other = 1.0 - same
    rows_same = same[:, tap_count:]
    rows_other = other[:, tap_count:]
    toeplitz = build_toeplitz(tap_rows)
    kv_same = same[:block_count] * windows
    kv_other = other[:block_count] * windows
    z_same = jnp.einsum('cij,cbj->cbi', toeplitz, kv_same, precision=lax.Precision.HIGHEST)
    z_other = jnp.einsum('cij,cbj->cbi', toeplitz, kv_other, precision=lax.Precision.HIGHEST)
    mixed = rows_same[:block_count] * z_same + rows_other[:block_count] * z_other
    g_blocks = g_ext.reshape(chan_count, block_count + 1, tap_count)
    g_same = rows_same * g_blocks
    g_other = rows_other * g_blocks
    d_same = jnp.einsum('cij,cbi->cbj', toeplitz, g_same, precision=lax.Precision.HIGHEST)
    d_other = jnp.einsum('cij,cbi->cbj', toeplitz, g_other, precision=lax.Precision.HIGHEST)
    d_win = same * d_same + other * d_other
    back = d_win[:, :block_count, tap_count:] + d_win[:, 1:, :tap_count]
    outer = jnp.einsum('cbi,cbj->cij', g_same[:, :block_count], kv_same, precision=lax.Precision.HIGHEST)
    outer = outer + jnp.einsum('cbi,cbj->cij', g_other[:, :block_count], kv_other, precision=lax.Precision.HIGHEST)
    row_count = block_count * tap_count
    return (mixed.reshape(chan_count, row_count), back.reshape(chan_count, row_count), lag_sums(outer))

def reference(query_act, key_act, value_act, out_grad, filter_taps, doc_ids):
    tap_count = filter_taps.shape[1]
    chan_count = filter_taps.shape[0]
    product = lax.optimization_barrier((key_act.astype(jnp.float32) * value_act.astype(jnp.float32)).astype(jnp.bfloat16))
    gated = lax.optimization_barrier((query_act.astype(jnp.float32) * out_grad.astype(jnp.float32)).astype(jnp.bfloat16))
    taps = lax.optimization_barrier(filter_taps.astype(jnp.bfloat16)).astype(jnp.float32)
    width = math.gcd(chan_count, 512)
    group_count = chan_count // width
    taps_groups = taps.reshape(group_count, width, tap_count)
    row_count = product.shape[0]
    kv_ext = jnp.concatenate([jnp.zeros((tap_count, chan_count), jnp.bfloat16), product], 0).T
    g_ext = jnp.concatenate([gated, jnp.zeros((tap_count, chan_count), jnp.bfloat16)], 0).T
    seg_ext = jnp.pad(doc_ids, (tap_count, tap_count))
    kv_groups = kv_ext.reshape(group_count, width, row_count + tap_count)
    g_groups = g_ext.reshape(group_count, width, row_count + tap_count)

    def one_group(parts):
        return mix_exact(parts[0].astype(jnp.float32), parts[1].astype(jnp.float32), seg_ext, parts[2])
    mixed, back, partial_value = lax.map(one_group, (kv_groups, g_groups, taps_groups))
    mixed = mixed.reshape(chan_count, row_count).T
    back = back.reshape(chan_count, row_count).T
    mixed = lax.optimization_barrier(mixed.astype(jnp.bfloat16)).astype(jnp.float32)
    back = lax.optimization_barrier(back.astype(jnp.bfloat16)).astype(jnp.float32)
    query_grad = (out_grad.astype(jnp.float32) * mixed).astype(jnp.bfloat16)
    key_grad = (back * value_act.astype(jnp.float32)).astype(jnp.bfloat16)
    value_grad = (back * key_act.astype(jnp.float32)).astype(jnp.bfloat16)
    filter_grad = partial_value.reshape(chan_count, tap_count) * (1.0 / math.sqrt(SEQ_LEN))
    return (query_grad, key_grad, value_grad, filter_grad)
```

```python
import functools
import math

import jax
import jax.numpy as jnp
import ml_dtypes
import numpy as np
from jax import lax
from jax.experimental import pallas as pl
from jax.experimental.pallas import tpu as pltpu
from jax.sharding import PartitionSpec as P

BOTH = ("dp", "ctx")
F32 = jnp.float32
BF16 = jnp.bfloat16


def split_bf16(matrix):
    high = matrix.astype(ml_dtypes.bfloat16)
    low = (matrix - high.astype(np.float64)).astype(ml_dtypes.bfloat16)
    return high, low


def transforms(count):
    freq = np.arange(count) + 0.5
    place = np.arange(count)

    def forward(offset):
        angle = np.pi / count * np.outer(freq, place + offset)
        high, low = split_bf16(np.concatenate([np.cos(angle), -np.sin(angle)], 0))
        return np.concatenate([high, low], 1)

    angle = np.pi / count * np.outer(place, freq)
    inverse = np.concatenate([np.cos(angle), -np.sin(angle)], 1) / count
    return forward(0), forward(-count), forward(count), split_bf16(inverse)


def dot(a, b):
    return jnp.dot(a, b, preferred_element_type=F32)


def doubled(block):
    return jnp.concatenate([block, block], 0)


def tap_spectrum(fwd, taps):
    both = jnp.concatenate([taps, taps], 1)
    return lax.dot_general(fwd, both, (((1,), (1,)), ((), ())), preferred_element_type=F32)


def halves(spectrum):
    count = spectrum.shape[0] // 2
    return spectrum[:count], spectrum[count:]


def times(a, b):
    ar, ai = halves(a)
    br, bi = halves(b)
    return jnp.concatenate([ar * br - ai * bi, ar * bi + ai * br], 0)


def times_conj(a, b):
    ar, ai = halves(a)
    br, bi = halves(b)
    return jnp.concatenate([ar * br + ai * bi, ai * br - ar * bi], 0)


def invert(inv, spectrum):
    out = dot(inv, spectrum.astype(BF16))
    count = out.shape[0] // 2
    return out[:count] + out[count:]


def masked(block, mask):
    return block * mask.astype(BF16)


def tiles(width, chans):
    tile = max(chans, min(width, 1024))
    return [(start, start + tile, range(start // chans, (start + tile) // chans)) for start in range(0, width, tile)]


def own_lags_kernel(x_ref, g_ref, masks_ref, fwd_ref, inv_ref, out_ref, sent_ref):
    first, rest = masks_ref[:, 0:1], masks_ref[:, 1:2]
    sent_ref[...] = g_ref[...]
    fwd = fwd_ref[...]
    chans = out_ref.shape[2]
    for start, stop, groups in tiles(x_ref.shape[1], chans):
        x, g = x_ref[:, start:stop], g_ref[:, start:stop]
        corr = times_conj(dot(fwd, doubled(masked(g, first))), dot(fwd, doubled(masked(x, first))))
        corr += times_conj(dot(fwd, doubled(masked(g, rest))), dot(fwd, doubled(masked(x, rest))))
        lags = invert(inv_ref[...], corr)
        for j, group in enumerate(groups):
            out_ref[group] = lags[:, j * chans : (j + 1) * chans]


def own_back_kernel(place_ref, g_ref, mine_ref, other_ref, masks_ref, fwd_ref, inv_ref, out_ref, taps_ref):
    first, rest = masks_ref[:, 0:1], masks_ref[:, 1:2]
    fwd, inv = fwd_ref[...], inv_ref[...]
    me, core = place_ref[0], place_ref[1]
    chans = 2 * mine_ref.shape[1]
    for start, stop, groups in tiles(g_ref.shape[1], chans):
        parts = []
        for group in groups:
            mine, other = mine_ref[group ^ me], other_ref[group ^ me]
            parts += [jnp.where(core == 0, mine, other), jnp.where(core == 0, other, mine)]
        taps = tap_spectrum(fwd, jnp.concatenate(parts, 0))
        taps_ref[:, start:stop] = taps
        g = g_ref[:, start:stop]
        head = invert(inv, times_conj(dot(fwd, doubled(masked(g, first))), taps))
        tail = invert(inv, times_conj(dot(fwd, doubled(masked(g, rest))), taps))
        out_ref[:, start:stop] = head * first + tail * rest


def lags_kernel(place_ref, g_ref, prior_ref, own_ref, masks_ref, fwd_ref, prior_fwd_ref, inv_ref, keep_ref, send_ref):
    first, before = masks_ref[:, 0:1], masks_ref[:, 2:3]
    chans = own_ref.shape[2]
    half = own_ref.shape[1] // 2
    me = place_ref[0]
    for start, stop, groups in tiles(g_ref.shape[1], chans):
        g = dot(fwd_ref[...], doubled(masked(g_ref[:, start:stop], first)))
        prior = dot(prior_fwd_ref[...], doubled(masked(prior_ref[:, start:stop], before)))
        lags = invert(inv_ref[...], times_conj(g, prior))
        for j, group in enumerate(groups):
            total = own_ref[group] + lags[:, j * chans : (j + 1) * chans]
            keep_ref[group ^ me] = total[:half]
            send_ref[group ^ me] = total[half:].astype(send_ref.dtype)


def query_kernel(x_ref, prior_ref, o_ref, taps_ref, masks_ref, fwd_ref, prior_fwd_ref, inv_ref, out_ref):
    first, rest, before = masks_ref[:, 0:1], masks_ref[:, 1:2], masks_ref[:, 2:3]
    fwd, inv = fwd_ref[...], inv_ref[...]
    for start, stop, _ in tiles(x_ref.shape[1], 1):
        x = x_ref[:, start:stop]
        taps = taps_ref[:, start:stop]
        prior = dot(prior_fwd_ref[...], doubled(masked(prior_ref[:, start:stop], before)))
        head = invert(inv, times(dot(fwd, doubled(masked(x, first))) + prior, taps))
        tail = invert(inv, times(dot(fwd, doubled(masked(x, rest))), taps))
        mixed = head * first + tail * rest
        out_ref[:, start:stop] = (o_ref[:, start:stop].astype(F32) * mixed).astype(out_ref.dtype)


def back_kernel(next_ref, own_ref, k_ref, v_ref, taps_ref, masks_ref, next_fwd_ref, inv_ref, k_out, v_out):
    after, last = masks_ref[:, 3:4], masks_ref[:, 4:5]
    for start, stop, _ in tiles(k_ref.shape[1], 1):
        later = dot(next_fwd_ref[...], doubled(masked(next_ref[:, start:stop], after)))
        later = invert(inv_ref[...], times_conj(later, taps_ref[:, start:stop]))
        back = own_ref[:, start:stop] + last * later
        k_out[:, start:stop] = (back * v_ref[:, start:stop].astype(F32)).astype(k_out.dtype)
        v_out[:, start:stop] = (back * k_ref[:, start:stop].astype(F32)).astype(v_out.dtype)


def first_sum_kernel(keep_ref, swapped_ref, own_ref, *send_refs):
    own_ref[...] = keep_ref[:2] + swapped_ref[:2].astype(F32)
    for j, send_ref in enumerate(send_refs):
        at = slice(2 * j + 2, 2 * j + 4)
        send_ref[...] = (keep_ref[at] + swapped_ref[at].astype(F32)).astype(send_ref.dtype)


def second_sum_kernel(count, *refs):
    total = refs[0][...]
    for ref in refs[1:count]:
        total = total + ref[...].astype(F32)
    own_ref, low_ref, high_ref = refs[count:]
    own_ref[...] = total[0]
    low_ref[...] = total[0].astype(low_ref.dtype)
    high_ref[...] = total[1].astype(high_ref.dtype)


def third_sum_kernel(count, *refs):
    total = refs[0][...]
    for ref in refs[1:count]:
        total = total + ref[...].astype(F32)
    for ref in refs[count:]:
        ref[...] = total


def finish_kernel(scale, place_ref, mine_ref, other_ref, out_ref):
    mine, other = mine_ref[...], other_ref[...]
    core = place_ref[1]
    low = jnp.where(core == 0, mine, other)
    high = jnp.where(core == 0, other, mine)
    out_ref[...] = jnp.concatenate([low, high], 0).T * scale


def swap(value, axis, bit):
    count = lax.axis_size(axis)
    return lax.ppermute(value, axis, [(i, i ^ bit) for i in range(count)])


def cross(value, dp_bits, ctx_bits):
    dp, ctx = lax.axis_size("dp"), lax.axis_size("ctx")
    pairs = [(d * ctx + c, (d ^ dp_bits) * ctx + (c ^ ctx_bits)) for d in range(dp) for c in range(ctx)]
    return lax.ppermute(value, BOTH, pairs)


def bits_of(count):
    assert count & (count - 1) == 0
    return [1 << b for b in range(count.bit_length() - 1)]


def gather_taps(taps):
    dp, ctx = lax.axis_size("dp"), lax.axis_size("ctx")
    core = lax.axis_index("dp") % 2
    chans = taps.shape[0]
    half = lax.dynamic_slice_in_dim(taps, core * (chans // 2), chans // 2, 0).astype(BF16)[None]
    steps = []
    for bit in bits_of(ctx):
        half = jnp.concatenate([half, swap(half, "ctx", bit)], 0)
        steps.append(half)
    return half, swap(half, "dp", 1), steps


def document_masks(doc_ids, rows):
    index = lax.axis_index(BOTH)
    padded = jnp.pad(doc_ids, (rows, rows), constant_values=-1)
    window = lax.dynamic_slice_in_dim(padded, index * rows, 3 * rows).reshape(3, rows)
    own = window[1]
    first = own == own[0]
    last = own == own[-1]
    before = window[0] == own[0]
    after = window[2] == own[-1]
    columns = [first, ~first, before, after, last, last, last, last]
    return jnp.stack(columns, 1).astype(F32)


def shards(query_act, key_act, value_act, out_grad, filter_taps, doc_ids):
    rows, width = query_act.shape
    chans, tap_count = filter_taps.shape
    dp, ctx = lax.axis_size("dp"), lax.axis_size("ctx")
    assert rows == tap_count and chans * ctx == width
    scale = 1.0 / math.sqrt(doc_ids.shape[0])
    count = dp * ctx
    fwd, prior_fwd, next_fwd, (inv_high, inv_low) = transforms(tap_count)
    inv = np.concatenate([inv_high, inv_low], 0)
    rolled = [np.concatenate([np.roll(m, -c * rows // 2, 0) for m in (inv_high, inv_low)], 0) for c in (0, 1)]
    core = lax.axis_index("dp") % 2
    inv_lags = lax.dynamic_index_in_dim(jnp.asarray(np.stack(rolled)), core, 0, keepdims=False)
    fwd, prior_fwd, next_fwd, inv = map(jnp.asarray, (fwd, prior_fwd, next_fwd, inv))

    place = jnp.stack([lax.axis_index("ctx"), core]).astype(jnp.int32)
    x = (key_act.astype(F32) * value_act.astype(F32)).astype(BF16)
    prior = lax.ppermute(x, BOTH, [(i, i + 1) for i in range(count - 1)])
    g = (query_act.astype(F32) * out_grad.astype(F32)).astype(BF16)
    taps_mine, taps_other, steps = gather_taps(filter_taps)
    masks = document_masks(doc_ids, rows)

    vmem = pl.BlockSpec(memory_space=pltpu.VMEM)
    smem = pl.BlockSpec(memory_space=pltpu.SMEM)
    anywhere = pl.BlockSpec(memory_space=pl.ANY)
    streamed = pl.BlockSpec()

    def call(kernel, outs, *args, scalars=0, after=(), out_specs=None):
        read = len(args)
        return pl.pallas_call(
            lambda *refs: kernel(*refs[:read], *refs[read + len(after) :]),
            out_shape=outs,
            in_specs=[smem] * scalars + [vmem] * (read - scalars) + [anywhere] * len(after),
            out_specs=jax.tree.map(lambda _: vmem, outs) if out_specs is None else out_specs,
            compiler_params=pltpu.CompilerParams(vmem_limit_bytes=40 * 1024 * 1024),
            cost_estimate=pl.CostEstimate(flops=1, bytes_accessed=1, transcendentals=0),
        )(*args, *after)

    sds = jax.ShapeDtypeStruct
    act = sds((rows, width), BF16)
    own_lags, g_sent = call(
        own_lags_kernel, (sds((ctx, rows, chans), F32), act), x, g, masks, fwd, inv_lags, after=(steps[1],),
        out_specs=(vmem, streamed),
    )
    later = lax.ppermute(g_sent, BOTH, [(i + 1, i) for i in range(count - 1)])
    keep, send = call(
        lags_kernel,
        (sds((ctx, rows // 2, chans), F32), sds((ctx, rows // 2, chans), BF16)),
        place, g, prior, own_lags, masks, fwd, prior_fwd, inv_lags,
        scalars=1, after=(steps[-1],), out_specs=(vmem, streamed),
    )
    own_back, spectrum = call(
        own_back_kernel,
        (sds((rows, width), F32), sds((2 * rows, width), F32)),
        place, g, taps_mine, taps_other, masks, fwd, inv,
        scalars=1, after=(send,),
    )
    query_grad = call(query_kernel, act, x, prior, out_grad, spectrum, masks, fwd, prior_fwd, inv)
    key_grad, value_grad = call(
        back_kernel, (act, act), later, own_back, key_act, value_act, spectrum, masks, next_fwd, inv
    )

    near = [j for j in range(2, ctx, 2)]
    pair = (2, rows // 2, chans)
    own, *sends = call(
        first_sum_kernel,
        (sds(pair, F32),) + (sds(pair, BF16),) * len(near),
        keep, swap(send, "dp", 1),
        out_specs=(vmem,) + (streamed,) * len(near),
    )
    got = [swap(value, "ctx", j) for value, j in zip(sends, near)]
    single = pair[1:]
    own, low, high = call(
        functools.partial(second_sum_kernel, 1 + len(got)),
        (sds(single, F32), sds(single, BF16), sds(single, BF16)),
        own, *got,
        out_specs=(vmem, streamed, streamed),
    )
    got = [
        cross(high if j else low, d, j) for d in range(0, dp, 2) for j in (0, 1) if d or j
    ]
    total, total_sent = call(
        functools.partial(third_sum_kernel, 1 + len(got)),
        (sds(single, F32), sds(single, F32)),
        own, *got,
        out_specs=(vmem, streamed),
    )
    filter_grad = call(
        functools.partial(finish_kernel, scale), sds((chans, tap_count), F32), place, total, swap(total_sent, "dp", 1),
        scalars=1,
    )
    return (query_grad, key_grad, value_grad, filter_grad)


def solution(mesh):
    in_specs = (
        P(BOTH, None),
        P(BOTH, None),
        P(BOTH, None),
        P(BOTH, None),
        P("ctx", None),
        P(),
    )
    out_specs = (
        P(BOTH, None),
        P(BOTH, None),
        P(BOTH, None),
        P("ctx", None),
    )
    return jax.shard_map(shards, mesh=mesh, in_specs=in_specs, out_specs=out_specs, check_vma=False)
```

```python
import functools
import math

import jax
import jax.numpy as jnp
import ml_dtypes
import numpy as np
from jax import lax
from jax.experimental import pallas as pl
from jax.experimental.pallas import tpu as pltpu
from jax.sharding import PartitionSpec as P

BOTH = ("dp", "ctx")
F32 = jnp.float32
BF16 = jnp.bfloat16


def split_bf16(matrix):
    high = matrix.astype(ml_dtypes.bfloat16)
    low = (matrix - high.astype(np.float64)).astype(ml_dtypes.bfloat16)
    return high, low


def transforms(count):
    freq = np.arange(count) + 0.5
    place = np.arange(count)

    def forward(offset):
        angle = np.pi / count * np.outer(freq, place + offset)
        high, low = split_bf16(np.concatenate([np.cos(angle), -np.sin(angle)], 0))
        return np.concatenate([high, low], 1)

    angle = np.pi / count * np.outer(place, freq)
    inverse = np.concatenate([np.cos(angle), -np.sin(angle)], 1) / count
    return forward(0), forward(-count), forward(count), split_bf16(inverse)


def dot(a, b):
    return jnp.dot(a, b, preferred_element_type=F32)


def doubled(block):
    return jnp.concatenate([block, block], 0)


def tap_spectrum(fwd, taps):
    both = jnp.concatenate([taps, taps], 1)
    return lax.dot_general(fwd, both, (((1,), (1,)), ((), ())), preferred_element_type=F32)


def halves(spectrum):
    count = spectrum.shape[0] // 2
    return spectrum[:count], spectrum[count:]


def times(a, b):
    ar, ai = halves(a)
    br, bi = halves(b)
    return jnp.concatenate([ar * br - ai * bi, ar * bi + ai * br], 0)


def times_conj(a, b):
    ar, ai = halves(a)
    br, bi = halves(b)
    return jnp.concatenate([ar * br + ai * bi, ai * br - ar * bi], 0)


def invert(inv, *spectra):
    out = dot(inv, jnp.concatenate([spectrum.astype(BF16) for spectrum in spectra], 0))
    count = out.shape[0] // 2
    return out[:count] + out[count:]


def masked(block, mask):
    return block * mask.astype(BF16)


def masked_inverse(inv, *masks):
    return jnp.concatenate([masked(inv, doubled(mask)) for mask in masks], 1)


def tiles(width, chans):
    tile = max(chans, 1024)
    spans = [(start, min(start + tile, width)) for start in range(0, width, tile)]
    return [(start, stop, range(start // chans, stop // chans)) for start, stop in spans]


def pick(flag, one, other):
    return jnp.where(flag != 0, one, other)


def product(a, b):
    return (a.astype(F32) * b.astype(F32)).astype(BF16)


def my_ctx():
    return lax.axis_index("ctx")


def my_quarter():
    return lax.axis_index("dp") % 4


def my_core():
    return lax.axis_index("dp") % 2


def my_parity():
    return lax.axis_index("ctx") % 2


def start_copy(flag, one, other, target, sem):
    @pl.when(flag != 0)
    def _():
        pltpu.make_async_copy(one, target, sem).start()

    @pl.when(flag == 0)
    def _():
        pltpu.make_async_copy(other, target, sem).start()


def store_when(flag, value, one_ref, other_ref, at):
    @pl.when(flag != 0)
    def _():
        one_ref[:, at] = value

    @pl.when(flag == 0)
    def _():
        other_ref[:, at] = value


def prelude_kernel(
    q_ref, k_ref, v_ref, o_ref, taps_ref, pair_ref, cross_ref, quarter_ref, bufs, tap_buf, sems, tap_sem
):
    split = pair_ref.shape[1]
    share = tap_buf.shape[0]
    rows = pl.ds(pl.multiple_of(my_quarter() * share, share), share)
    tap_copy = pltpu.make_async_copy(taps_ref.at[rows, :], tap_buf, tap_sem)
    spans = tiles(split, 1)
    copies = []
    for i, (start, stop, _) in enumerate(spans):
        at, high = slice(start, stop), slice(split + start, split + stop)
        parts = (k_ref.at[:, at], v_ref.at[:, at], q_ref.at[:, high], o_ref.at[:, high])
        copies.append([pltpu.make_async_copy(part, bufs.at[j, :, at], sems.at[j, i]) for j, part in enumerate(parts)])
    tap_copy.start()
    for group in copies:
        for copy in group:
            copy.start()
    tap_copy.wait()
    quarter_ref[0] = tap_buf[...].astype(quarter_ref.dtype)
    for group, (start, stop, _) in zip(copies, spans):
        at = slice(start, stop)
        for copy in group:
            copy.wait()
        store_when(my_parity(), product(bufs[0, :, at], bufs[1, :, at]), cross_ref, pair_ref, at)
        store_when(my_parity(), product(bufs[2, :, at], bufs[3, :, at]), pair_ref, cross_ref, at)


def masks_kernel(held_ref, docs_ref, out_ref, sent_ref):
    sent_ref[...] = held_ref[...]
    count, rows = docs_ref.shape
    index = lax.axis_index(BOTH)
    own = docs_ref[pl.ds(index, 1), :]
    before = docs_ref[pl.ds(jnp.maximum(index - 1, 0), 1), :]
    after = docs_ref[pl.ds(jnp.minimum(index + 1, count - 1), 1), :]
    first = own == own[:, 0:1]
    last = own == own[:, rows - 1 : rows]
    before = (before == own[:, 0:1]) & (index > 0)
    after = (after == own[:, rows - 1 : rows]) & (index < count - 1)
    lines = [jnp.where(line, 1.0, 0.0) for line in (first, ~first, before, after, last, last, last, last)]
    out_ref[...] = jnp.concatenate(lines, 0).T


def spectra_kernel(
    q_ref, k_ref, v_ref, o_ref, masks_ref, fwd_ref, inv_ref, taps_in,
    lags_ref, xa_ref, xb_ref, ga_ref, gb_ref, pair_ref, cross_ref, taps_out,
):
    taps_out[...] = taps_in[...]
    first, rest = masks_ref[:, 0:1], masks_ref[:, 1:2]
    fwd = fwd_ref[...]
    odd, split = my_parity(), pair_ref.shape[1]
    for start, stop, _ in tiles(lags_ref.shape[1], 1):
        at = slice(start, stop)
        x, g = product(k_ref[:, at], v_ref[:, at]), product(q_ref[:, at], o_ref[:, at])
        if start < split:
            store_when(odd, g, pair_ref, cross_ref, at)
        else:
            store_when(odd, x, cross_ref, pair_ref, slice(start - split, stop - split))
        xa, ga = dot(fwd, doubled(masked(x, first))), dot(fwd, doubled(masked(g, first)))
        xb, gb = dot(fwd, doubled(masked(x, rest))), dot(fwd, doubled(masked(g, rest)))
        xa_ref[:, at], ga_ref[:, at] = xa, ga
        xb_ref[:, at], gb_ref[:, at] = xb, gb
        lags_ref[:, at] = invert(inv_ref[...], times_conj(ga, xa) + times_conj(gb, xb))


def fetch_halo(odd, spans, low_if_odd, low_if_even, halo_ref, sems):
    split = low_if_odd.shape[1]
    for i, (start, stop, _) in enumerate(spans):
        target, sem = halo_ref.at[:, start:stop], sems.at[i]
        if start < split:
            start_copy(odd, low_if_odd.at[:, start:stop], low_if_even.at[:, start:stop], target, sem)
        else:
            high = slice(start - split, stop - split)
            start_copy(odd, low_if_even.at[:, high], low_if_odd.at[:, high], target, sem)

    def wait(i):
        start, stop, _ = spans[i]
        pltpu.make_async_copy(low_if_odd.at[:, 0 : stop - start], halo_ref.at[:, start:stop], sems.at[i]).wait()

    return wait


def lags_kernel(
    pair_ref, cross_ref, held_ref, own_ref, xa_ref, xb_ref, ga_ref, masks_ref,
    prior_fwd_ref, next_fwd_ref, inv_ref, keep_ref, halo_ref, send_ref, sent_ref, sems,
):
    sent_ref[...] = held_ref[...]
    rows = masks_ref.shape[0]
    before, after = masks_ref[:, 2:3], masks_ref[:, 3:4]
    single = masks_ref[rows - 1 : rows, 0:1] > 0.0
    chans, half = keep_ref.shape[2], keep_ref.shape[1]
    me, core = my_ctx(), my_core()
    split = pair_ref.shape[1]
    spans = tiles(2 * split, chans)
    wait = fetch_halo(my_parity(), spans, pair_ref, cross_ref, halo_ref, sems)
    for i, (start, stop, groups) in enumerate(spans):
        at = slice(start, stop)
        wait(i)
        if start < split:
            prior = dot(prior_fwd_ref[...], doubled(masked(halo_ref[:, at], before)))
            spectrum = times_conj(ga_ref[:, at], prior)
        else:
            later = dot(next_fwd_ref[...], doubled(masked(halo_ref[:, at], after)))
            spectrum = times_conj(later, jnp.where(single, xa_ref[:, at], xb_ref[:, at]))
        lags = own_ref[:, at] + invert(inv_ref[...], spectrum)
        low, high = lags[:half], lags[half:]
        keep, send = pick(core, high, low), pick(core, low, high)
        for j, group in enumerate(groups):
            keep_ref[group ^ me] = keep[:, j * chans : (j + 1) * chans]
            send_ref[group ^ me] = send[:, j * chans : (j + 1) * chans].astype(send_ref.dtype)


def middle_kernel(
    halo_ref, k_ref, v_ref, o_ref, xa_ref, xb_ref, ga_ref, gb_ref, mine_ref, other_ref,
    masks_ref, fwd_ref, prior_fwd_ref, next_fwd_ref, inv_ref,
    taps_ref, mixed_ref, back_ref, q_out, k_out, v_out,
):
    first, rest, before, after, last = (masks_ref[:, i : i + 1] for i in range(5))
    inv_two = masked_inverse(inv_ref[...], first, rest)
    inv_three = masked_inverse(inv_ref[...], first, rest, last)
    me, quarter = my_ctx(), my_quarter()
    split = q_out.shape[1]
    chans = 4 * mine_ref.shape[2]
    for start, stop, groups in tiles(2 * split, chans):
        parts = []
        for group in groups:
            for r in range(4):
                place = (r ^ quarter) // 2, group ^ me
                parts.append(pick((r ^ quarter) % 2, other_ref[place], mine_ref[place]))
        at = slice(start, stop)
        taps = tap_spectrum(fwd_ref[...], jnp.concatenate(parts, 0))
        taps_ref[:, at] = taps
        halo = halo_ref[:, at]
        xa, xb, ga, gb = (ref[:, at] for ref in (xa_ref, xb_ref, ga_ref, gb_ref))
        if start < split:
            prior = dot(prior_fwd_ref[...], doubled(masked(halo, before)))
            mixed = invert(inv_two, times(xa + prior, taps), times(xb, taps))
            q_out[:, at] = (o_ref[:, at].astype(F32) * mixed).astype(q_out.dtype)
            back_ref[:, at] = invert(inv_two, times_conj(ga, taps), times_conj(gb, taps))
        else:
            mine = slice(start - split, stop - split)
            later = dot(next_fwd_ref[...], doubled(masked(halo, after)))
            mixed_ref[:, mine] = invert(inv_two, times(xa, taps), times(xb, taps))
            back = invert(inv_three, times_conj(ga, taps), times_conj(gb, taps), times_conj(later, taps))
            k_out[:, mine] = (back * v_ref[:, at].astype(F32)).astype(k_out.dtype)
            v_out[:, mine] = (back * k_ref[:, at].astype(F32)).astype(v_out.dtype)


def last_kernel(
    pair_ref, cross_ref, k_ref, v_ref, o_ref, taps_ref, mixed_ref, back_ref, q_half, k_half, v_half,
    masks_ref, prior_fwd_ref, next_fwd_ref, inv_ref, q_out, k_out, v_out, halo_ref, sems,
):
    first, before, after, last = (masks_ref[:, i : i + 1] for i in (0, 2, 3, 4))
    inv_first = masked_inverse(inv_ref[...], first)
    inv_last = masked_inverse(inv_ref[...], last)
    split = pair_ref.shape[1]
    spans = tiles(2 * split, 1)
    wait = fetch_halo(my_parity(), spans, cross_ref, pair_ref, halo_ref, sems)
    q_out[:, :split] = q_half[...]
    k_out[:, split:] = k_half[...]
    v_out[:, split:] = v_half[...]
    for i, (start, stop, _) in enumerate(spans):
        at = slice(start, stop)
        taps = taps_ref[:, at]
        wait(i)
        if start < split:
            later = dot(next_fwd_ref[...], doubled(masked(halo_ref[:, at], after)))
            back = back_ref[:, at] + invert(inv_last, times_conj(later, taps))
            k_out[:, at] = (back * v_ref[:, at].astype(F32)).astype(k_out.dtype)
            v_out[:, at] = (back * k_ref[:, at].astype(F32)).astype(v_out.dtype)
        else:
            prior = dot(prior_fwd_ref[...], doubled(masked(halo_ref[:, at], before)))
            mixed = mixed_ref[:, start - split : stop - split] + invert(inv_first, times(prior, taps))
            q_out[:, at] = (o_ref[:, at].astype(F32) * mixed).astype(q_out.dtype)


def first_sum_kernel(keep_ref, swapped_ref, own_ref, *send_refs):
    own_ref[...] = keep_ref[:2] + swapped_ref[:2].astype(F32)
    for j, send_ref in enumerate(send_refs):
        at = slice(2 * j + 2, 2 * j + 4)
        send_ref[...] = (keep_ref[at] + swapped_ref[at].astype(F32)).astype(send_ref.dtype)


def second_sum_kernel(count, *refs):
    total = refs[0][...]
    for ref in refs[1:count]:
        total = total + ref[...].astype(F32)
    own_ref, low_ref, high_ref = refs[count:]
    own_ref[...] = total[0]
    low_ref[...] = total[0].astype(low_ref.dtype)
    high_ref[...] = total[1].astype(high_ref.dtype)


def third_sum_kernel(count, *refs):
    total = refs[0][...]
    for ref in refs[1:count]:
        total = total + ref[...].astype(F32)
    for ref in refs[count:]:
        ref[...] = total


def finish_kernel(scale, mine_ref, other_ref, out_ref):
    mine, other = mine_ref[...], other_ref[...]
    core = my_core()
    low = jnp.where(core == 0, mine, other)
    high = jnp.where(core == 0, other, mine)
    out_ref[...] = jnp.concatenate([low, high], 0).T * scale


def swap(value, axis, bit):
    count = lax.axis_size(axis)
    return lax.ppermute(value, axis, [(i, i ^ bit) for i in range(count)])


def cross(value, dp_bits, ctx_bits):
    dp, ctx = lax.axis_size("dp"), lax.axis_size("ctx")
    pairs = [(d * ctx + c, (d ^ dp_bits) * ctx + (c ^ ctx_bits)) for d in range(dp) for c in range(ctx)]
    return lax.ppermute(value, BOTH, pairs)


def bits_of(count):
    assert count & (count - 1) == 0
    return [1 << b for b in range(count.bit_length() - 1)]


def gather_near_taps(mine):
    pair = jnp.concatenate([mine, swap(mine, "ctx", 1)], 0)
    return jnp.concatenate([pair] + [swap(pair, "ctx", j) for j in range(2, lax.axis_size("ctx"), 2)], 0)


def gather_far_taps(near):
    both = jnp.stack([near, swap(near, "dp", 2)])
    return both, swap(both, "dp", 1)


def shards(query_act, key_act, value_act, out_grad, filter_taps, doc_ids):
    rows, width = query_act.shape
    chans, tap_count = filter_taps.shape
    dp, ctx = lax.axis_size("dp"), lax.axis_size("ctx")
    assert rows == tap_count and chans * ctx == width
    scale = 1.0 / math.sqrt(doc_ids.shape[0])
    count = dp * ctx
    fwd, prior_fwd, next_fwd, (inv_high, inv_low) = transforms(tap_count)
    inv = np.concatenate([inv_high, inv_low], 0)
    fwd, prior_fwd, next_fwd, inv = map(jnp.asarray, (fwd, prior_fwd, next_fwd, inv))

    split = width // 2
    pairs = [(i, i ^ 1) for i in range(count)]
    crosses = [(i, i + 1 if i % 2 else i - 1) for i in range(1, count - 1)]
    vmem = pl.BlockSpec(memory_space=pltpu.VMEM)
    anywhere = pl.BlockSpec(memory_space=pl.ANY)
    hbm = pl.BlockSpec(memory_space=pltpu.HBM)
    streamed = pl.BlockSpec()

    def call(kernel, outs, *args, after=(), direct=0, out_specs=None, scratch=(), limit=8):
        read = len(args)
        return pl.pallas_call(
            lambda *refs: kernel(*refs[:read], *refs[read + len(after) :]),
            out_shape=outs,
            in_specs=[hbm] * direct + [vmem] * (read - direct) + [anywhere] * len(after),
            out_specs=jax.tree.map(lambda _: vmem, outs) if out_specs is None else out_specs,
            scratch_shapes=scratch,
            compiler_params=pltpu.CompilerParams(vmem_limit_bytes=limit * 1024 * 1024),
            cost_estimate=pl.CostEstimate(flops=1, bytes_accessed=1, transcendentals=0),
        )(*args, *after)

    sds = jax.ShapeDtypeStruct
    act = sds((rows, width), BF16)
    full = sds((2 * rows, width), F32)
    half_act = sds((rows, split), BF16)
    half_sum = sds((rows, split), F32)
    n_tiles = len(tiles(width, chans))
    buffer = pltpu.VMEM((rows, width), BF16)

    share = chans // 4
    acts = (query_act, key_act, value_act, out_grad)
    sent, held, taps_quarter = call(
        prelude_kernel,
        (half_act, half_act, sds((1, share, tap_count), BF16)),
        *acts, filter_taps,
        direct=5, out_specs=(streamed, vmem, streamed),
        scratch=[
            pltpu.VMEM((4, rows, split), BF16),
            pltpu.VMEM((share, tap_count), F32),
            pltpu.SemaphoreType.DMA((4, n_tiles)),
            pltpu.SemaphoreType.DMA,
        ],
        limit=60,
    )
    pair_early = lax.ppermute(sent, BOTH, pairs)
    taps_near = gather_near_taps(taps_quarter)
    masks, sent = call(
        masks_kernel,
        (sds((rows, 8), F32), half_act),
        held, doc_ids.reshape(-1, rows),
        after=(taps_near, pair_early), out_specs=(vmem, streamed),
    )
    cross_early = lax.ppermute(sent, BOTH, crosses)
    own_lags, xa, xb, ga, gb, held, sent, taps_near = call(
        spectra_kernel,
        (sds((rows, width), F32), full, full, full, full, half_act, half_act, sds(taps_near.shape, BF16)),
        *acts, masks, fwd, inv, taps_near,
        after=(pair_early,), out_specs=(vmem,) * 6 + (streamed,) * 2, limit=16,
    )
    cross_late = lax.ppermute(sent, BOTH, crosses)
    taps_mine, taps_other = gather_far_taps(taps_near)
    keep, halo, send, sent = call(
        lags_kernel,
        (sds((ctx, rows // 2, chans), F32), act, sds((ctx, rows // 2, chans), BF16), half_act),
        pair_early, cross_early, held, own_lags, xa, xb, ga, masks, prior_fwd, next_fwd, inv,
        direct=2, out_specs=(vmem, vmem, streamed, streamed),
        scratch=[pltpu.SemaphoreType.DMA((n_tiles,))], limit=12,
    )
    pair_late = lax.ppermute(sent, BOTH, pairs)
    spectrum, own_mixed, own_back, query_half, key_half, value_half = call(
        middle_kernel,
        (full, half_sum, half_sum, half_act, half_act, half_act),
        halo, key_act, value_act, out_grad, xa, xb, ga, gb, taps_mine, taps_other,
        masks, fwd, prior_fwd, next_fwd, inv,
        after=(send,), limit=16,
    )

    near = [j for j in range(2, ctx, 2)]
    pair = (2, rows // 2, chans)
    own, *sends = call(
        first_sum_kernel,
        (sds(pair, F32),) + (sds(pair, BF16),) * len(near),
        keep, swap(send, "dp", 1),
        after=(cross_late,), out_specs=(vmem,) + (streamed,) * len(near),
    )
    got = [swap(value, "ctx", j) for value, j in zip(sends, near)]
    query_grad, key_grad, value_grad = call(
        last_kernel,
        (act, act, act),
        pair_late, cross_late, key_act, value_act, out_grad, spectrum, own_mixed, own_back,
        query_half, key_half, value_half, masks, prior_fwd, next_fwd, inv,
        direct=2, scratch=[buffer, pltpu.SemaphoreType.DMA((n_tiles,))], limit=12,
    )
    piece = pair[1:]
    own, low, high = call(
        functools.partial(second_sum_kernel, 1 + len(got)),
        (sds(piece, F32), sds(piece, BF16), sds(piece, BF16)),
        own, *got,
        after=(query_half,), out_specs=(vmem, streamed, streamed),
    )
    got = [
        cross(high if j else low, d, j) for d in range(0, dp, 2) for j in (0, 1) if d or j
    ]
    total, total_sent = call(
        functools.partial(third_sum_kernel, 1 + len(got)),
        (sds(piece, F32), sds(piece, F32)),
        own, *got,
        out_specs=(vmem, streamed),
    )
    filter_grad = call(
        functools.partial(finish_kernel, scale), sds((chans, tap_count), F32), total, swap(total_sent, "dp", 1),
    )
    return (query_grad, key_grad, value_grad, filter_grad)


def solution(mesh):
    in_specs = (
        P(BOTH, None),
        P(BOTH, None),
        P(BOTH, None),
        P(BOTH, None),
        P("ctx", None),
        P(),
    )
    out_specs = (
        P(BOTH, None),
        P(BOTH, None),
        P(BOTH, None),
        P("ctx", None),
    )
    return jax.shard_map(shards, mesh=mesh, in_specs=in_specs, out_specs=out_specs, check_vma=False)
```

```python
import functools
import math

import jax
import jax.numpy as jnp
import ml_dtypes
import numpy as np
from jax import lax
from jax.experimental import pallas as pl
from jax.experimental.pallas import tpu as pltpu
from jax.sharding import PartitionSpec as P

BOTH = ("dp", "ctx")
F32 = jnp.float32
BF16 = jnp.bfloat16


def split_bf16(matrix):
    high = matrix.astype(ml_dtypes.bfloat16)
    low = (matrix - high.astype(np.float64)).astype(ml_dtypes.bfloat16)
    return high, low


def transforms(count):
    freq = np.arange(count) + 0.5
    place = np.arange(count)

    def forward(offset):
        angle = np.pi / count * np.outer(freq, place + offset)
        high, low = split_bf16(np.concatenate([np.cos(angle), -np.sin(angle)], 0))
        return np.concatenate([high, low], 1)

    angle = np.pi / count * np.outer(place, freq)
    inverse = np.concatenate([np.cos(angle), -np.sin(angle)], 1) / count
    return forward(0), forward(-count), forward(count), split_bf16(inverse)


def dot(a, b):
    return jnp.dot(a, b, preferred_element_type=F32)


def doubled(block):
    return jnp.concatenate([block, block], 0)


def tap_spectrum(fwd, taps):
    both = jnp.concatenate([taps, taps], 1)
    return lax.dot_general(fwd, both, (((1,), (1,)), ((), ())), preferred_element_type=F32)


def halves(spectrum):
    count = spectrum.shape[0] // 2
    return spectrum[:count], spectrum[count:]


def times(a, b):
    ar, ai = halves(a)
    br, bi = halves(b)
    return jnp.concatenate([ar * br - ai * bi, ar * bi + ai * br], 0)


def times_conj(a, b):
    ar, ai = halves(a)
    br, bi = halves(b)
    return jnp.concatenate([ar * br + ai * bi, ai * br - ar * bi], 0)


def invert(inv, *spectra):
    out = dot(inv, jnp.concatenate([spectrum.astype(BF16) for spectrum in spectra], 0))
    count = out.shape[0] // 2
    return out[:count] + out[count:]


def masked(block, mask):
    return block * mask.astype(BF16)


def masked_inverse(inv, *masks):
    return jnp.concatenate([masked(inv, doubled(mask)) for mask in masks], 1)


def tiles(width, chans):
    tile = max(chans, 1024)
    spans = [(start, min(start + tile, width)) for start in range(0, width, tile)]
    return [(start, stop, range(start // chans, stop // chans)) for start, stop in spans]


def pick(flag, one, other):
    return jnp.where(flag != 0, one, other)


def product(a, b):
    return (a.astype(F32) * b.astype(F32)).astype(BF16)


def my_ctx():
    return lax.axis_index("ctx")


def my_quarter():
    return lax.axis_index("dp") % 4


def my_core():
    return lax.axis_index("dp") % 2


def my_parity():
    return lax.axis_index("ctx") % 2


def start_copy(flag, one, other, target, sem):
    @pl.when(flag != 0)
    def _():
        pltpu.make_async_copy(one, target, sem).start()

    @pl.when(flag == 0)
    def _():
        pltpu.make_async_copy(other, target, sem).start()


def prelude_kernel(
    q_ref, k_ref, v_ref, o_ref, taps_ref, pair_ref, quarter_ref, a_buf, b_buf, tap_buf, sems, tap_sem
):
    split = pair_ref.shape[1]
    share = tap_buf.shape[0]
    rows = pl.ds(pl.multiple_of(my_quarter() * share, share), share)
    tap_copy = pltpu.make_async_copy(taps_ref.at[rows, :], tap_buf, tap_sem)
    spans = tiles(split, 1)
    odd = my_parity()
    for i, (start, stop, _) in enumerate(spans):
        at, high = slice(start, stop), slice(split + start, split + stop)
        start_copy(odd, q_ref.at[:, high], k_ref.at[:, at], a_buf.at[:, at], sems.at[0, i])
        start_copy(odd, o_ref.at[:, high], v_ref.at[:, at], b_buf.at[:, at], sems.at[1, i])
    tap_copy.start()
    for i, (start, stop, _) in enumerate(spans):
        at = slice(start, stop)
        pltpu.make_async_copy(k_ref.at[:, at], a_buf.at[:, at], sems.at[0, i]).wait()
        pltpu.make_async_copy(v_ref.at[:, at], b_buf.at[:, at], sems.at[1, i]).wait()
        pair_ref[:, at] = product(a_buf[:, at], b_buf[:, at])
    tap_copy.wait()
    quarter_ref[0] = tap_buf[...].astype(quarter_ref.dtype)


def cross_kernel(q_ref, k_ref, v_ref, o_ref, cross_ref):
    split = cross_ref.shape[1]
    for start, stop, _ in tiles(split, 1):
        low, high = slice(start, stop), slice(split + start, split + stop)

        @pl.when(my_parity() != 0)
        def _():
            cross_ref[:, low] = product(k_ref[:, low], v_ref[:, low])

        @pl.when(my_parity() == 0)
        def _():
            cross_ref[:, low] = product(q_ref[:, high], o_ref[:, high])


def late_kernel(q_ref, k_ref, v_ref, o_ref, docs_ref, masks_ref, pair_ref, cross_ref):
    split = cross_ref.shape[1]
    for start, stop, _ in tiles(split, 1):
        low, high = slice(start, stop), slice(split + start, split + stop)
        store_when(my_parity(), product(k_ref[:, high], v_ref[:, high]), cross_ref, pair_ref, low)
        store_when(my_parity(), product(q_ref[:, low], o_ref[:, low]), pair_ref, cross_ref, low)
    count, rows = docs_ref.shape
    index = lax.axis_index(BOTH)
    own = docs_ref[pl.ds(index, 1), :]
    before = docs_ref[pl.ds(jnp.maximum(index - 1, 0), 1), :]
    after = docs_ref[pl.ds(jnp.minimum(index + 1, count - 1), 1), :]
    first = own == own[:, 0:1]
    last = own == own[:, rows - 1 : rows]
    before = (before == own[:, 0:1]) & (index > 0)
    after = (after == own[:, rows - 1 : rows]) & (index < count - 1)
    lines = [jnp.where(line, 1.0, 0.0) for line in (first, ~first, before, after, last, last, last, last)]
    masks_ref[...] = jnp.concatenate(lines, 0).T


def store_when(flag, value, one_ref, other_ref, at):
    @pl.when(flag != 0)
    def _():
        one_ref[:, at] = value

    @pl.when(flag == 0)
    def _():
        other_ref[:, at] = value


def spectra_kernel(
    q_ref, k_ref, v_ref, o_ref, masks_ref, fwd_ref, inv_ref, lags_ref, xa_ref, xb_ref, ga_ref, gb_ref
):
    first, rest = masks_ref[:, 0:1], masks_ref[:, 1:2]
    fwd = fwd_ref[...]
    for start, stop, _ in tiles(lags_ref.shape[1], 1):
        at = slice(start, stop)
        x, g = product(k_ref[:, at], v_ref[:, at]), product(q_ref[:, at], o_ref[:, at])
        xa, ga = dot(fwd, doubled(masked(x, first))), dot(fwd, doubled(masked(g, first)))
        xb, gb = dot(fwd, doubled(masked(x, rest))), dot(fwd, doubled(masked(g, rest)))
        xa_ref[:, at], ga_ref[:, at] = xa, ga
        xb_ref[:, at], gb_ref[:, at] = xb, gb
        lags_ref[:, at] = invert(inv_ref[...], times_conj(ga, xa) + times_conj(gb, xb))


def fetch_halo(odd, spans, low_if_odd, low_if_even, halo_ref, sems):
    split = low_if_odd.shape[1]
    for i, (start, stop, _) in enumerate(spans):
        target, sem = halo_ref.at[:, start:stop], sems.at[i]
        if start < split:
            start_copy(odd, low_if_odd.at[:, start:stop], low_if_even.at[:, start:stop], target, sem)
        else:
            high = slice(start - split, stop - split)
            start_copy(odd, low_if_even.at[:, high], low_if_odd.at[:, high], target, sem)

    def wait(i):
        start, stop, _ = spans[i]
        pltpu.make_async_copy(low_if_odd.at[:, 0 : stop - start], halo_ref.at[:, start:stop], sems.at[i]).wait()

    return wait


def lags_kernel(
    pair_ref, cross_ref, own_ref, xa_ref, xb_ref, ga_ref, masks_ref,
    prior_fwd_ref, next_fwd_ref, inv_ref, keep_ref, halo_ref, *rest,
):
    *sends, sems = rest
    rows = masks_ref.shape[0]
    before, after = masks_ref[:, 2:3], masks_ref[:, 3:4]
    single = masks_ref[rows - 1 : rows, 0:1] > 0.0
    chans, half = keep_ref.shape[2], keep_ref.shape[1]
    me, core = my_ctx(), my_core()
    split = pair_ref.shape[1]
    spans = tiles(2 * split, chans)
    wait = fetch_halo(my_parity(), spans, pair_ref, cross_ref, halo_ref, sems)
    for i, (start, stop, groups) in enumerate(spans):
        at = slice(start, stop)
        wait(i)
        if start < split:
            prior = dot(prior_fwd_ref[...], doubled(masked(halo_ref[:, at], before)))
            spectrum = times_conj(ga_ref[:, at], prior)
        else:
            later = dot(next_fwd_ref[...], doubled(masked(halo_ref[:, at], after)))
            spectrum = times_conj(later, jnp.where(single, xa_ref[:, at], xb_ref[:, at]))
        lags = own_ref[:, at] + invert(inv_ref[...], spectrum)
        low, high = lags[:half], lags[half:]
        keep, send = pick(core, high, low), pick(core, low, high)
        for j, group in enumerate(groups):
            keep_ref[group ^ me] = keep[:, j * chans : (j + 1) * chans]
            place, value = group ^ me, send[:, j * chans : (j + 1) * chans].astype(BF16)
            for near, send_ref in enumerate(sends):

                @pl.when(place // 2 == near)
                def _(send_ref=send_ref):
                    send_ref[place % 2] = value


def middle_kernel(
    halo_ref, k_ref, v_ref, o_ref, xa_ref, xb_ref, ga_ref, gb_ref, near_ref, far_ref, other_near_ref, other_far_ref,
    masks_ref, fwd_ref, prior_fwd_ref, next_fwd_ref, inv_ref,
    taps_ref, mixed_ref, back_ref, q_out, k_out, v_out,
):
    first, rest, before, after, last = (masks_ref[:, i : i + 1] for i in range(5))
    inv_two = masked_inverse(inv_ref[...], first, rest)
    inv_three = masked_inverse(inv_ref[...], first, rest, last)
    me, quarter = my_ctx(), my_quarter()
    split = q_out.shape[1]
    shares = (near_ref, far_ref), (other_near_ref, other_far_ref)
    chans = 4 * near_ref.shape[1]
    for start, stop, groups in tiles(2 * split, chans):
        parts = []
        for group in groups:
            for r in range(4):
                place = r ^ quarter
                mine, other = (pick(place // 2, far[group ^ me], near[group ^ me]) for near, far in shares)
                parts.append(pick(place % 2, other, mine))
        at = slice(start, stop)
        taps = tap_spectrum(fwd_ref[...], jnp.concatenate(parts, 0))
        taps_ref[:, at] = taps
        halo = halo_ref[:, at]
        xa, xb, ga, gb = (ref[:, at] for ref in (xa_ref, xb_ref, ga_ref, gb_ref))
        if start < split:
            prior = dot(prior_fwd_ref[...], doubled(masked(halo, before)))
            mixed = invert(inv_two, times(xa + prior, taps), times(xb, taps))
            q_out[:, at] = (o_ref[:, at].astype(F32) * mixed).astype(q_out.dtype)
            back_ref[:, at] = invert(inv_two, times_conj(ga, taps), times_conj(gb, taps))
        else:
            mine = slice(start - split, stop - split)
            later = dot(next_fwd_ref[...], doubled(masked(halo, after)))
            mixed_ref[:, mine] = invert(inv_two, times(xa, taps), times(xb, taps))
            back = invert(inv_three, times_conj(ga, taps), times_conj(gb, taps), times_conj(later, taps))
            k_out[:, mine] = (back * v_ref[:, at].astype(F32)).astype(k_out.dtype)
            v_out[:, mine] = (back * k_ref[:, at].astype(F32)).astype(v_out.dtype)


def last_kernel(
    pair_ref, cross_ref, k_ref, v_ref, o_ref, taps_ref, mixed_ref, back_ref, q_half, k_half, v_half,
    masks_ref, prior_fwd_ref, next_fwd_ref, inv_ref, q_out, k_out, v_out, mark_ref,
    halo_ref, q_buf, k_buf, v_buf, sems, out_sems,
):
    mark_ref[...] = jnp.zeros_like(mark_ref)
    first, before, after, last = (masks_ref[:, i : i + 1] for i in (0, 2, 3, 4))
    inv_first = masked_inverse(inv_ref[...], first)
    inv_last = masked_inverse(inv_ref[...], last)
    split = pair_ref.shape[1]
    spans = tiles(2 * split, 1)
    wait = fetch_halo(my_parity(), spans, cross_ref, pair_ref, halo_ref, sems)
    copies = []

    def send(source, target):
        copies.append(pltpu.make_async_copy(source, target, out_sems.at[len(copies)]))
        copies[-1].start()

    send(q_half, q_out.at[:, :split])
    send(k_half, k_out.at[:, split:])
    send(v_half, v_out.at[:, split:])
    for i, (start, stop, _) in enumerate(spans):
        at = slice(start, stop)
        taps = taps_ref[:, at]
        wait(i)
        if start < split:
            later = dot(next_fwd_ref[...], doubled(masked(halo_ref[:, at], after)))
            back = back_ref[:, at] + invert(inv_last, times_conj(later, taps))
            k_buf[:, at] = (back * v_ref[:, at].astype(F32)).astype(k_buf.dtype)
            v_buf[:, at] = (back * k_ref[:, at].astype(F32)).astype(v_buf.dtype)
            send(k_buf.at[:, at], k_out.at[:, at])
            send(v_buf.at[:, at], v_out.at[:, at])
        else:
            mine = slice(start - split, stop - split)
            prior = dot(prior_fwd_ref[...], doubled(masked(halo_ref[:, at], before)))
            mixed = mixed_ref[:, mine] + invert(inv_first, times(prior, taps))
            q_buf[:, mine] = (o_ref[:, at].astype(F32) * mixed).astype(q_buf.dtype)
            send(q_buf.at[:, mine], q_out.at[:, at])
    for copy in copies:
        copy.wait()


def first_sum_kernel(count, keep_ref, *refs):
    for j, (swapped_ref, out_ref) in enumerate(zip(refs[:count], refs[count:])):
        out_ref[...] = (keep_ref[2 * j : 2 * j + 2] + swapped_ref[...].astype(F32)).astype(out_ref.dtype)


def second_sum_kernel(count, *refs):
    total = refs[0][...]
    for ref in refs[1:count]:
        total = total + ref[...].astype(F32)
    own_ref, low_ref, high_ref = refs[count:]
    own_ref[...] = total[0]
    low_ref[...] = total[0].astype(low_ref.dtype)
    high_ref[...] = total[1].astype(high_ref.dtype)


def third_sum_kernel(count, *refs):
    total = refs[0][...]
    for ref in refs[1:count]:
        total = total + ref[...].astype(F32)
    for ref in refs[count:]:
        ref[...] = total


def finish_kernel(scale, mine_ref, other_ref, out_ref):
    mine, other = mine_ref[...], other_ref[...]
    core = my_core()
    low = jnp.where(core == 0, mine, other)
    high = jnp.where(core == 0, other, mine)
    out_ref[...] = jnp.concatenate([low, high], 0).T * scale


def swap(value, axis, bit):
    count = lax.axis_size(axis)
    return lax.ppermute(value, axis, [(i, i ^ bit) for i in range(count)])


def cross(value, dp_bits, ctx_bits):
    dp, ctx = lax.axis_size("dp"), lax.axis_size("ctx")
    pairs = [(d * ctx + c, (d ^ dp_bits) * ctx + (c ^ ctx_bits)) for d in range(dp) for c in range(ctx)]
    return lax.ppermute(value, BOTH, pairs)


def bits_of(count):
    assert count & (count - 1) == 0
    return [1 << b for b in range(count.bit_length() - 1)]


def gather_near_taps(mine):
    pair = jnp.concatenate([mine, swap(mine, "ctx", 1)], 0)
    return jnp.concatenate([pair] + [swap(pair, "ctx", j) for j in range(2, lax.axis_size("ctx"), 2)], 0)


def gather_far_taps(near):
    far = swap(near, "dp", 2)
    return near, far, swap(near, "dp", 1), swap(far, "dp", 1)


def shards(query_act, key_act, value_act, out_grad, filter_taps, doc_ids):
    rows, width = query_act.shape
    chans, tap_count = filter_taps.shape
    dp, ctx = lax.axis_size("dp"), lax.axis_size("ctx")
    assert rows == tap_count and chans * ctx == width
    scale = 1.0 / math.sqrt(doc_ids.shape[0])
    count = dp * ctx
    fwd, prior_fwd, next_fwd, (inv_high, inv_low) = transforms(tap_count)
    inv = np.concatenate([inv_high, inv_low], 0)
    fwd, prior_fwd, next_fwd, inv = map(jnp.asarray, (fwd, prior_fwd, next_fwd, inv))

    split = width // 2
    pairs = [(i, i ^ 1) for i in range(count)]
    crosses = [(i, i + 1 if i % 2 else i - 1) for i in range(1, count - 1)]
    vmem = pl.BlockSpec(memory_space=pltpu.VMEM)
    anywhere = pl.BlockSpec(memory_space=pl.ANY)
    hbm = pl.BlockSpec(memory_space=pltpu.HBM)
    streamed = pl.BlockSpec()

    def call(kernel, outs, *args, after=(), direct=0, out_specs=None, scratch=(), limit=8, flops=1):
        read = len(args)
        return pl.pallas_call(
            lambda *refs: kernel(*refs[:read], *refs[read + len(after) :]),
            out_shape=outs,
            in_specs=[hbm] * direct + [vmem] * (read - direct) + [anywhere] * len(after),
            out_specs=jax.tree.map(lambda _: vmem, outs) if out_specs is None else out_specs,
            scratch_shapes=scratch,
            compiler_params=pltpu.CompilerParams(vmem_limit_bytes=limit * 1024 * 1024),
            cost_estimate=pl.CostEstimate(flops=flops, bytes_accessed=1, transcendentals=0),
        )(*args, *after)

    sds = jax.ShapeDtypeStruct
    act = sds((rows, width), BF16)
    full = sds((2 * rows, width), F32)
    half_act = sds((rows, split), BF16)
    half_sum = sds((rows, split), F32)
    n_tiles = len(tiles(width, chans))
    buffer = pltpu.VMEM((rows, width), BF16)

    share = chans // 4
    acts = (query_act, key_act, value_act, out_grad)
    sent, taps_quarter = call(
        prelude_kernel,
        (half_act, sds((1, share, tap_count), BF16)),
        *acts, filter_taps,
        direct=5, out_specs=(vmem, vmem),
        scratch=[
            pltpu.VMEM((rows, split), BF16),
            pltpu.VMEM((rows, split), BF16),
            pltpu.VMEM((share, tap_count), F32),
            pltpu.SemaphoreType.DMA((2, n_tiles)),
            pltpu.SemaphoreType.DMA,
        ],
        limit=56,
    )
    pair_early = lax.ppermute(sent, BOTH, pairs)
    taps_near = gather_near_taps(taps_quarter)
    sent = call(cross_kernel, half_act, *acts, after=(taps_near, pair_early), out_specs=streamed)
    cross_early = lax.ppermute(sent, BOTH, crosses)
    masks, pair_sent, cross_sent = call(
        late_kernel,
        (sds((rows, 8), F32), half_act, half_act),
        *acts, doc_ids.reshape(-1, rows),
        after=(sent,), out_specs=(vmem, streamed, streamed),
    )
    cross_late = lax.ppermute(cross_sent, BOTH, crosses)
    pair_late = lax.ppermute(pair_sent, BOTH, pairs)
    taps_all = gather_far_taps(taps_near)
    own_lags, xa, xb, ga, gb = call(
        spectra_kernel,
        (sds((rows, width), F32), full, full, full, full),
        *acts, masks, fwd, inv,
        limit=16,
    )
    pair = (2, rows // 2, chans)
    keep, halo, *sends = call(
        lags_kernel,
        (sds((ctx, rows // 2, chans), F32), act) + (sds(pair, BF16),) * (ctx // 2),
        pair_early, cross_early, own_lags, xa, xb, ga, masks, prior_fwd, next_fwd, inv,
        direct=2, out_specs=(vmem, vmem) + (streamed,) * (ctx // 2),
        scratch=[pltpu.SemaphoreType.DMA((n_tiles,))], limit=12,
    )
    spectrum, own_mixed, own_back, query_half, key_half, value_half = call(
        middle_kernel,
        (full, half_sum, half_sum, half_act, half_act, half_act),
        halo, key_act, value_act, out_grad, xa, xb, ga, gb, *taps_all,
        masks, fwd, prior_fwd, next_fwd, inv,
        after=(sends[0], cross_late), limit=16,
    )

    near = [j for j in range(2, ctx, 2)]
    own, *sends = call(
        functools.partial(first_sum_kernel, ctx // 2),
        (sds(pair, F32),) + (sds(pair, BF16),) * len(near),
        keep, *(swap(value, "dp", 1) for value in sends),
        out_specs=(vmem,) + (streamed,) * len(near),
    )
    got = [swap(value, "ctx", j) for value, j in zip(sends, near)]
    query_grad, key_grad, value_grad, mark = call(
        last_kernel,
        (act, act, act, sds((8, 128), F32)),
        pair_late, cross_late, key_act, value_act, out_grad, spectrum, own_mixed, own_back,
        query_half, key_half, value_half, masks, prior_fwd, next_fwd, inv,
        direct=2, out_specs=(hbm, hbm, hbm, vmem), limit=14,
        scratch=[buffer]
        + [pltpu.VMEM((rows, split), BF16)] * 3
        + [pltpu.SemaphoreType.DMA((n_tiles,)), pltpu.SemaphoreType.DMA((3 + 2 * n_tiles,))],
    )
    piece = pair[1:]
    own, low, high = call(
        functools.partial(second_sum_kernel, 1 + len(got)),
        (sds(piece, F32), sds(piece, BF16), sds(piece, BF16)),
        own, *got,
        after=(query_half,), out_specs=(vmem, streamed, streamed),
    )
    got = [
        cross(high if j else low, d, j) for d in reversed(range(0, dp, 2)) for j in (1, 0) if d or j
    ]
    total, total_sent = call(
        functools.partial(third_sum_kernel, 1 + len(got)),
        (sds(piece, F32), sds(piece, F32)),
        own, *got,
        after=(mark,), out_specs=(vmem, streamed),
    )
    filter_grad = call(
        functools.partial(finish_kernel, scale), sds((chans, tap_count), F32), total, swap(total_sent, "dp", 1),
    )
    return (query_grad, key_grad, value_grad, filter_grad)


def solution(mesh):
    in_specs = (
        P(BOTH, None),
        P(BOTH, None),
        P(BOTH, None),
        P(BOTH, None),
        P("ctx", None),
        P(),
    )
    out_specs = (
        P(BOTH, None),
        P(BOTH, None),
        P(BOTH, None),
        P("ctx", None),
    )
    return jax.shard_map(shards, mesh=mesh, in_specs=in_specs, out_specs=out_specs, check_vma=False)
```

```python
import functools
import math

import jax
import jax.numpy as jnp
import ml_dtypes
import numpy as np
from jax import lax
from jax.experimental import pallas as pl
from jax.experimental.pallas import tpu as pltpu
from jax.sharding import PartitionSpec as P

BOTH = ("dp", "ctx")
F32 = jnp.float32
BF16 = jnp.bfloat16


def split_bf16(matrix):
    high = matrix.astype(ml_dtypes.bfloat16)
    low = (matrix - high.astype(np.float64)).astype(ml_dtypes.bfloat16)
    return high, low


def transforms(count):
    freq = np.arange(count) + 0.5
    place = np.arange(count)

    def forward(offset):
        angle = np.pi / count * np.outer(freq, place + offset)
        high, low = split_bf16(np.concatenate([np.cos(angle), -np.sin(angle)], 0))
        return np.concatenate([high, low], 1)

    angle = np.pi / count * np.outer(place, freq)
    inverse = np.concatenate([np.cos(angle), -np.sin(angle)], 1) / count
    return forward(0), forward(-count), forward(count), split_bf16(inverse)


def dot(a, b):
    return jnp.dot(a, b, preferred_element_type=F32)


def doubled(block):
    return jnp.concatenate([block, block], 0)


def tap_spectrum(fwd, taps):
    both = jnp.concatenate([taps, taps], 1)
    return lax.dot_general(fwd, both, (((1,), (1,)), ((), ())), preferred_element_type=F32)


def halves(spectrum):
    count = spectrum.shape[0] // 2
    return spectrum[:count], spectrum[count:]


def times(a, b):
    ar, ai = halves(a)
    br, bi = halves(b)
    return jnp.concatenate([ar * br - ai * bi, ar * bi + ai * br], 0)


def times_conj(a, b):
    ar, ai = halves(a)
    br, bi = halves(b)
    return jnp.concatenate([ar * br + ai * bi, ai * br - ar * bi], 0)


def invert(inv, *spectra):
    out = dot(inv, jnp.concatenate([spectrum.astype(BF16) for spectrum in spectra], 0))
    count = out.shape[0] // 2
    return out[:count] + out[count:]


def masked(block, mask):
    return block * mask.astype(BF16)


def masked_inverse(inv, *masks):
    return jnp.concatenate([masked(inv, doubled(mask)) for mask in masks], 1)


def tiles(width, chans):
    tile = max(chans, 1024)
    spans = [(start, min(start + tile, width)) for start in range(0, width, tile)]
    return [(start, stop, range(start // chans, stop // chans)) for start, stop in spans]


def pick(flag, one, other):
    return jnp.where(flag != 0, one, other)


def product(a, b):
    return (a.astype(F32) * b.astype(F32)).astype(BF16)


def my_ctx():
    return lax.axis_index("ctx")


def my_quarter():
    return lax.axis_index("dp") % 4


def my_core():
    return lax.axis_index("dp") % 2


def my_parity():
    return lax.axis_index("ctx") % 2


def start_copy(flag, one, other, target, sem):
    @pl.when(flag != 0)
    def _():
        pltpu.make_async_copy(one, target, sem).start()

    @pl.when(flag == 0)
    def _():
        pltpu.make_async_copy(other, target, sem).start()


def prelude_kernel(
    q_ref, k_ref, v_ref, o_ref, taps_ref, pair_ref, quarter_ref, a_buf, b_buf, tap_buf, sems, tap_sem
):
    split = pair_ref.shape[1]
    share = tap_buf.shape[0]
    rows = pl.ds(pl.multiple_of(my_quarter() * share, share), share)
    tap_copy = pltpu.make_async_copy(taps_ref.at[rows, :], tap_buf, tap_sem)
    spans = tiles(split, 1)
    odd = my_parity()
    for i, (start, stop, _) in enumerate(spans):
        at, high = slice(start, stop), slice(split + start, split + stop)
        start_copy(odd, q_ref.at[:, high], k_ref.at[:, at], a_buf.at[:, at], sems.at[0, i])
        start_copy(odd, o_ref.at[:, high], v_ref.at[:, at], b_buf.at[:, at], sems.at[1, i])
    tap_copy.start()
    for i, (start, stop, _) in enumerate(spans):
        at = slice(start, stop)
        pltpu.make_async_copy(k_ref.at[:, at], a_buf.at[:, at], sems.at[0, i]).wait()
        pltpu.make_async_copy(v_ref.at[:, at], b_buf.at[:, at], sems.at[1, i]).wait()
        pair_ref[:, at] = product(a_buf[:, at], b_buf[:, at])
    tap_copy.wait()
    quarter_ref[0] = tap_buf[...].astype(quarter_ref.dtype)


def cross_kernel(q_ref, k_ref, v_ref, o_ref, cross_ref):
    split = cross_ref.shape[1]
    for start, stop, _ in tiles(split, 1):
        low, high = slice(start, stop), slice(split + start, split + stop)

        @pl.when(my_parity() != 0)
        def _():
            cross_ref[:, low] = product(k_ref[:, low], v_ref[:, low])

        @pl.when(my_parity() == 0)
        def _():
            cross_ref[:, low] = product(q_ref[:, high], o_ref[:, high])


def late_kernel(q_ref, k_ref, v_ref, o_ref, docs_ref, masks_ref, pair_ref, cross_ref):
    split = cross_ref.shape[1]
    for start, stop, _ in tiles(split, 1):
        low, high = slice(start, stop), slice(split + start, split + stop)
        store_when(my_parity(), product(k_ref[:, high], v_ref[:, high]), cross_ref, pair_ref, low)
        store_when(my_parity(), product(q_ref[:, low], o_ref[:, low]), pair_ref, cross_ref, low)
    count, rows = docs_ref.shape
    index = lax.axis_index(BOTH)
    own = docs_ref[pl.ds(index, 1), :]
    before = docs_ref[pl.ds(jnp.maximum(index - 1, 0), 1), :]
    after = docs_ref[pl.ds(jnp.minimum(index + 1, count - 1), 1), :]
    first = own == own[:, 0:1]
    last = own == own[:, rows - 1 : rows]
    before = (before == own[:, 0:1]) & (index > 0)
    after = (after == own[:, rows - 1 : rows]) & (index < count - 1)
    lines = [jnp.where(line, 1.0, 0.0) for line in (first, ~first, before, after, last, last, last, last)]
    masks_ref[...] = jnp.concatenate(lines, 0).T


def store_when(flag, value, one_ref, other_ref, at):
    @pl.when(flag != 0)
    def _():
        one_ref[:, at] = value

    @pl.when(flag == 0)
    def _():
        other_ref[:, at] = value


def spectra_kernel(
    q_ref, k_ref, v_ref, o_ref, masks_ref, fwd_ref, inv_ref, lags_ref, xa_ref, xb_ref, ga_ref, gb_ref
):
    first, rest = masks_ref[:, 0:1], masks_ref[:, 1:2]
    fwd = fwd_ref[...]
    for start, stop, _ in tiles(lags_ref.shape[1], 1):
        at = slice(start, stop)
        x, g = product(k_ref[:, at], v_ref[:, at]), product(q_ref[:, at], o_ref[:, at])
        xa, ga = dot(fwd, doubled(masked(x, first))), dot(fwd, doubled(masked(g, first)))
        xb, gb = dot(fwd, doubled(masked(x, rest))), dot(fwd, doubled(masked(g, rest)))
        xa_ref[:, at], ga_ref[:, at] = xa, ga
        xb_ref[:, at], gb_ref[:, at] = xb, gb
        lags_ref[:, at] = invert(inv_ref[...], times_conj(ga, xa) + times_conj(gb, xb))


def halo_of(low_if_odd, low_if_even, start, stop):
    split = low_if_odd.shape[1]
    at = slice(start % split, start % split + stop - start)
    one, two = (low_if_odd, low_if_even) if start < split else (low_if_even, low_if_odd)
    return pick(my_parity(), one[:, at], two[:, at])


def lags_kernel(
    pair_ref, cross_ref, own_ref, xa_ref, xb_ref, ga_ref, masks_ref,
    prior_fwd_ref, next_fwd_ref, inv_ref, keep_ref, halo_ref, *sends,
):
    rows = masks_ref.shape[0]
    before, after = masks_ref[:, 2:3], masks_ref[:, 3:4]
    single = masks_ref[rows - 1 : rows, 0:1] > 0.0
    chans, half = keep_ref.shape[2], keep_ref.shape[1]
    me, core = my_ctx(), my_core()
    split = pair_ref.shape[1]
    spans = tiles(2 * split, chans)
    for start, stop, groups in spans:
        at = slice(start, stop)
        halo = halo_of(pair_ref, cross_ref, start, stop)
        halo_ref[:, at] = halo
        if start < split:
            prior = dot(prior_fwd_ref[...], doubled(masked(halo, before)))
            spectrum = times_conj(ga_ref[:, at], prior)
        else:
            later = dot(next_fwd_ref[...], doubled(masked(halo, after)))
            spectrum = times_conj(later, jnp.where(single, xa_ref[:, at], xb_ref[:, at]))
        lags = own_ref[:, at] + invert(inv_ref[...], spectrum)
        low, high = lags[:half], lags[half:]
        keep, send = pick(core, high, low), pick(core, low, high)
        for j, group in enumerate(groups):
            keep_ref[group ^ me] = keep[:, j * chans : (j + 1) * chans]
            place, value = group ^ me, send[:, j * chans : (j + 1) * chans].astype(BF16)
            for near, send_ref in enumerate(sends):

                @pl.when(place // 2 == near)
                def _(send_ref=send_ref):
                    send_ref[place % 2] = value


def middle_kernel(
    halo_ref, k_ref, v_ref, o_ref, xa_ref, xb_ref, ga_ref, gb_ref, near_ref, far_ref, other_near_ref, other_far_ref,
    masks_ref, fwd_ref, prior_fwd_ref, next_fwd_ref, inv_ref,
    taps_ref, mixed_ref, back_ref, q_out, k_out, v_out,
):
    first, rest, before, after, last = (masks_ref[:, i : i + 1] for i in range(5))
    inv_two = masked_inverse(inv_ref[...], first, rest)
    inv_three = masked_inverse(inv_ref[...], first, rest, last)
    me, quarter = my_ctx(), my_quarter()
    split = q_out.shape[1]
    shares = (near_ref, far_ref), (other_near_ref, other_far_ref)
    chans = 4 * near_ref.shape[1]
    for start, stop, groups in tiles(2 * split, chans):
        parts = []
        for group in groups:
            for r in range(4):
                place = r ^ quarter
                mine, other = (pick(place // 2, far[group ^ me], near[group ^ me]) for near, far in shares)
                parts.append(pick(place % 2, other, mine))
        at = slice(start, stop)
        taps = tap_spectrum(fwd_ref[...], jnp.concatenate(parts, 0))
        taps_ref[:, at] = taps
        halo = halo_ref[:, at]
        xa, xb, ga, gb = (ref[:, at] for ref in (xa_ref, xb_ref, ga_ref, gb_ref))
        if start < split:
            prior = dot(prior_fwd_ref[...], doubled(masked(halo, before)))
            mixed = invert(inv_two, times(xa + prior, taps), times(xb, taps))
            q_out[:, at] = (o_ref[:, at].astype(F32) * mixed).astype(q_out.dtype)
            back_ref[:, at] = invert(inv_two, times_conj(ga, taps), times_conj(gb, taps))
        else:
            mine = slice(start - split, stop - split)
            later = dot(next_fwd_ref[...], doubled(masked(halo, after)))
            mixed_ref[:, mine] = invert(inv_two, times(xa, taps), times(xb, taps))
            back = invert(inv_three, times_conj(ga, taps), times_conj(gb, taps), times_conj(later, taps))
            k_out[:, mine] = (back * v_ref[:, at].astype(F32)).astype(k_out.dtype)
            v_out[:, mine] = (back * k_ref[:, at].astype(F32)).astype(v_out.dtype)


def last_kernel(
    pair_ref, cross_ref, k_ref, v_ref, o_ref, taps_ref, mixed_ref, back_ref, q_half, k_half, v_half,
    masks_ref, prior_fwd_ref, next_fwd_ref, inv_ref, q_out, k_out, v_out, mark_ref,
    q_buf, k_buf, v_buf, out_sems,
):
    mark_ref[...] = jnp.zeros_like(mark_ref)
    first, before, after, last = (masks_ref[:, i : i + 1] for i in (0, 2, 3, 4))
    inv_first = masked_inverse(inv_ref[...], first)
    inv_last = masked_inverse(inv_ref[...], last)
    split = pair_ref.shape[1]
    spans = tiles(2 * split, 1)
    copies = []

    def send(source, target):
        copies.append(pltpu.make_async_copy(source, target, out_sems.at[len(copies)]))
        copies[-1].start()

    send(q_half, q_out.at[:, :split])
    send(k_half, k_out.at[:, split:])
    send(v_half, v_out.at[:, split:])
    for start, stop, _ in spans:
        at = slice(start, stop)
        taps = taps_ref[:, at]
        halo = halo_of(cross_ref, pair_ref, start, stop)
        if start < split:
            later = dot(next_fwd_ref[...], doubled(masked(halo, after)))
            back = back_ref[:, at] + invert(inv_last, times_conj(later, taps))
            k_buf[:, at] = (back * v_ref[:, at].astype(F32)).astype(k_buf.dtype)
            v_buf[:, at] = (back * k_ref[:, at].astype(F32)).astype(v_buf.dtype)
            send(k_buf.at[:, at], k_out.at[:, at])
            send(v_buf.at[:, at], v_out.at[:, at])
        else:
            mine = slice(start - split, stop - split)
            prior = dot(prior_fwd_ref[...], doubled(masked(halo, before)))
            mixed = mixed_ref[:, mine] + invert(inv_first, times(prior, taps))
            q_buf[:, mine] = (o_ref[:, at].astype(F32) * mixed).astype(q_buf.dtype)
            send(q_buf.at[:, mine], q_out.at[:, at])
    for copy in copies:
        copy.wait()


def first_sum_kernel(count, keep_ref, *refs):
    for j, (swapped_ref, out_ref) in enumerate(zip(refs[:count], refs[count:])):
        out_ref[...] = (keep_ref[2 * j : 2 * j + 2] + swapped_ref[...].astype(F32)).astype(out_ref.dtype)


def second_sum_kernel(count, *refs):
    total = refs[0][...]
    for ref in refs[1:count]:
        total = total + ref[...].astype(F32)
    own_ref, low_ref, high_ref = refs[count:]
    own_ref[...] = total[0]
    low_ref[...] = total[0].astype(low_ref.dtype)
    high_ref[...] = total[1].astype(high_ref.dtype)


def third_sum_kernel(count, *refs):
    total = refs[0][...]
    for ref in refs[1:count]:
        total = total + ref[...].astype(F32)
    for ref in refs[count:]:
        ref[...] = total


def finish_kernel(scale, mine_ref, other_ref, out_ref):
    mine, other = mine_ref[...], other_ref[...]
    core = my_core()
    low = jnp.where(core == 0, mine, other)
    high = jnp.where(core == 0, other, mine)
    out_ref[...] = jnp.concatenate([low, high], 0).T * scale


def swap(value, axis, bit):
    count = lax.axis_size(axis)
    return lax.ppermute(value, axis, [(i, i ^ bit) for i in range(count)])


def cross(value, dp_bits, ctx_bits):
    dp, ctx = lax.axis_size("dp"), lax.axis_size("ctx")
    pairs = [(d * ctx + c, (d ^ dp_bits) * ctx + (c ^ ctx_bits)) for d in range(dp) for c in range(ctx)]
    return lax.ppermute(value, BOTH, pairs)


def bits_of(count):
    assert count & (count - 1) == 0
    return [1 << b for b in range(count.bit_length() - 1)]


def gather_near_taps(mine):
    pair = jnp.concatenate([mine, swap(mine, "ctx", 1)], 0)
    return jnp.concatenate([pair] + [swap(pair, "ctx", j) for j in range(2, lax.axis_size("ctx"), 2)], 0)


def gather_far_taps(near):
    far = swap(near, "dp", 2)
    return near, far, swap(near, "dp", 1), swap(far, "dp", 1)


def shards(query_act, key_act, value_act, out_grad, filter_taps, doc_ids):
    rows, width = query_act.shape
    chans, tap_count = filter_taps.shape
    dp, ctx = lax.axis_size("dp"), lax.axis_size("ctx")
    assert rows == tap_count and chans * ctx == width
    scale = 1.0 / math.sqrt(doc_ids.shape[0])
    count = dp * ctx
    fwd, prior_fwd, next_fwd, (inv_high, inv_low) = transforms(tap_count)
    inv = np.concatenate([inv_high, inv_low], 0)
    fwd, prior_fwd, next_fwd, inv = map(jnp.asarray, (fwd, prior_fwd, next_fwd, inv))

    split = width // 2
    pairs = [(i, i ^ 1) for i in range(count)]
    crosses = [(i, i + 1 if i % 2 else i - 1) for i in range(1, count - 1)]
    vmem = pl.BlockSpec(memory_space=pltpu.VMEM)
    anywhere = pl.BlockSpec(memory_space=pl.ANY)
    hbm = pl.BlockSpec(memory_space=pltpu.HBM)
    streamed = pl.BlockSpec()

    def call(kernel, outs, *args, after=(), direct=0, out_specs=None, scratch=(), limit=8, flops=1):
        read = len(args)
        return pl.pallas_call(
            lambda *refs: kernel(*refs[:read], *refs[read + len(after) :]),
            out_shape=outs,
            in_specs=[hbm] * direct + [vmem] * (read - direct) + [anywhere] * len(after),
            out_specs=jax.tree.map(lambda _: vmem, outs) if out_specs is None else out_specs,
            scratch_shapes=scratch,
            compiler_params=pltpu.CompilerParams(vmem_limit_bytes=limit * 1024 * 1024),
            cost_estimate=pl.CostEstimate(flops=flops, bytes_accessed=1, transcendentals=0),
        )(*args, *after)

    sds = jax.ShapeDtypeStruct
    act = sds((rows, width), BF16)
    full = sds((2 * rows, width), F32)
    half_act = sds((rows, split), BF16)
    half_sum = sds((rows, split), F32)
    n_tiles = len(tiles(width, chans))

    share = chans // 4
    acts = (query_act, key_act, value_act, out_grad)
    sent, taps_quarter = call(
        prelude_kernel,
        (half_act, sds((1, share, tap_count), BF16)),
        *acts, filter_taps,
        direct=5, out_specs=(vmem, vmem),
        scratch=[
            pltpu.VMEM((rows, split), BF16),
            pltpu.VMEM((rows, split), BF16),
            pltpu.VMEM((share, tap_count), F32),
            pltpu.SemaphoreType.DMA((2, n_tiles)),
            pltpu.SemaphoreType.DMA,
        ],
        limit=56,
    )
    pair_early = lax.ppermute(sent, BOTH, pairs)
    taps_near = gather_near_taps(taps_quarter)
    sent = call(cross_kernel, half_act, *acts, after=(taps_near, pair_early), out_specs=streamed)
    cross_early = lax.ppermute(sent, BOTH, crosses)
    masks, pair_sent, cross_sent = call(
        late_kernel,
        (sds((rows, 8), F32), half_act, half_act),
        *acts, doc_ids.reshape(-1, rows),
        after=(sent,), out_specs=(vmem, streamed, streamed),
    )
    cross_late = lax.ppermute(cross_sent, BOTH, crosses)
    pair_late = lax.ppermute(pair_sent, BOTH, pairs)
    taps_all = gather_far_taps(taps_near)
    own_lags, xa, xb, ga, gb = call(
        spectra_kernel,
        (sds((rows, width), F32), full, full, full, full),
        *acts, masks, fwd, inv,
        limit=16,
    )
    pair = (2, rows // 2, chans)
    keep, halo, *sends = call(
        lags_kernel,
        (sds((ctx, rows // 2, chans), F32), act) + (sds(pair, BF16),) * (ctx // 2),
        pair_early, cross_early, own_lags, xa, xb, ga, masks, prior_fwd, next_fwd, inv,
        out_specs=(vmem, vmem) + (streamed,) * (ctx // 2), limit=12,
    )
    spectrum, own_mixed, own_back, query_half, key_half, value_half = call(
        middle_kernel,
        (full, half_sum, half_sum, half_act, half_act, half_act),
        halo, key_act, value_act, out_grad, xa, xb, ga, gb, *taps_all,
        masks, fwd, prior_fwd, next_fwd, inv,
        after=(sends[0], cross_late), limit=16,
    )

    near = [j for j in range(2, ctx, 2)]
    own, *sends = call(
        functools.partial(first_sum_kernel, ctx // 2),
        (sds(pair, F32),) + (sds(pair, BF16),) * len(near),
        keep, *(swap(value, "dp", 1) for value in sends),
        out_specs=(vmem,) + (streamed,) * len(near),
    )
    got = [swap(value, "ctx", j) for value, j in zip(sends, near)]
    query_grad, key_grad, value_grad, mark = call(
        last_kernel,
        (act, act, act, sds((8, 128), F32)),
        pair_late, cross_late, key_act, value_act, out_grad, spectrum, own_mixed, own_back,
        query_half, key_half, value_half, masks, prior_fwd, next_fwd, inv,
        out_specs=(hbm, hbm, hbm, vmem), limit=14,
        scratch=[pltpu.VMEM((rows, split), BF16)] * 3 + [pltpu.SemaphoreType.DMA((3 + 2 * n_tiles,))],
    )
    piece = pair[1:]
    own, low, high = call(
        functools.partial(second_sum_kernel, 1 + len(got)),
        (sds(piece, F32), sds(piece, BF16), sds(piece, BF16)),
        own, *got,
        after=(query_half,), out_specs=(vmem, streamed, streamed),
    )
    got = [
        cross(high if j else low, d, j) for d in reversed(range(0, dp, 2)) for j in (1, 0) if d or j
    ]
    total, total_sent = call(
        functools.partial(third_sum_kernel, 1 + len(got)),
        (sds(piece, F32), sds(piece, F32)),
        own, *got,
        after=(mark,), out_specs=(vmem, streamed),
    )
    filter_grad = call(
        functools.partial(finish_kernel, scale), sds((chans, tap_count), F32), total, swap(total_sent, "dp", 1),
    )
    return (query_grad, key_grad, value_grad, filter_grad)


def solution(mesh):
    in_specs = (
        P(BOTH, None),
        P(BOTH, None),
        P(BOTH, None),
        P(BOTH, None),
        P("ctx", None),
        P(),
    )
    out_specs = (
        P(BOTH, None),
        P(BOTH, None),
        P(BOTH, None),
        P("ctx", None),
    )
    return jax.shard_map(shards, mesh=mesh, in_specs=in_specs, out_specs=out_specs, check_vma=False)
```

```python
import functools
import math

import jax
import jax.numpy as jnp
import ml_dtypes
import numpy as np
from jax import lax
from jax.experimental import pallas as pl
from jax.experimental.pallas import tpu as pltpu
from jax.sharding import PartitionSpec as P

BOTH = ("dp", "ctx")
F32 = jnp.float32
BF16 = jnp.bfloat16


def split_bf16(matrix):
    high = matrix.astype(ml_dtypes.bfloat16)
    low = (matrix - high.astype(np.float64)).astype(ml_dtypes.bfloat16)
    return high, low


def transforms(count):
    freq = np.arange(count) + 0.5
    place = np.arange(count)

    def forward(offset):
        angle = np.pi / count * np.outer(freq, place + offset)
        high, low = split_bf16(np.concatenate([np.cos(angle), -np.sin(angle)], 0))
        return np.concatenate([high, low], 1)

    angle = np.pi / count * np.outer(place, freq)
    inverse = np.concatenate([np.cos(angle), -np.sin(angle)], 1) / count
    return forward(0), forward(-count), forward(count), split_bf16(inverse)


def dot(a, b):
    return jnp.dot(a, b, preferred_element_type=F32)


def doubled(block):
    return jnp.concatenate([block, block], 0)


def tap_spectrum(fwd, taps):
    both = jnp.concatenate([taps, taps], 1)
    return lax.dot_general(fwd, both, (((1,), (1,)), ((), ())), preferred_element_type=F32)


def halves(spectrum):
    count = spectrum.shape[0] // 2
    return spectrum[:count], spectrum[count:]


def times(a, b):
    ar, ai = halves(a)
    br, bi = halves(b)
    return jnp.concatenate([ar * br - ai * bi, ar * bi + ai * br], 0)


def times_conj(a, b):
    ar, ai = halves(a)
    br, bi = halves(b)
    return jnp.concatenate([ar * br + ai * bi, ai * br - ar * bi], 0)


def invert(inv, *spectra):
    out = dot(inv, jnp.concatenate([spectrum.astype(BF16) for spectrum in spectra], 0))
    count = out.shape[0] // 2
    return out[:count] + out[count:]


def masked(block, mask):
    return block * mask.astype(BF16)


def masked_inverse(inv, *masks):
    return jnp.concatenate([masked(inv, doubled(mask)) for mask in masks], 1)


def tiles(width, chans):
    tile = max(chans, 1024)
    spans = [(start, min(start + tile, width)) for start in range(0, width, tile)]
    return [(start, stop, range(start // chans, stop // chans)) for start, stop in spans]


def pick(flag, one, other):
    return jnp.where(flag != 0, one, other)


def product(a, b):
    return (a.astype(F32) * b.astype(F32)).astype(BF16)


def my_ctx():
    return lax.axis_index("ctx")


def my_quarter():
    return lax.axis_index("dp") % 4


def my_core():
    return lax.axis_index("dp") % 2


def my_parity():
    return lax.axis_index("ctx") % 2


def start_copy(flag, one, other, target, sem):
    @pl.when(flag != 0)
    def _():
        pltpu.make_async_copy(one, target, sem).start()

    @pl.when(flag == 0)
    def _():
        pltpu.make_async_copy(other, target, sem).start()


def prelude_kernel(
    q_ref, k_ref, v_ref, o_ref, taps_ref, pair_ref, quarter_ref, a_buf, b_buf, tap_buf, sems, tap_sem
):
    split = pair_ref.shape[1]
    share = tap_buf.shape[0]
    rows = pl.ds(pl.multiple_of(my_quarter() * share, share), share)
    tap_copy = pltpu.make_async_copy(taps_ref.at[rows, :], tap_buf, tap_sem)
    spans = tiles(split, 1)
    odd = my_parity()
    for i, (start, stop, _) in enumerate(spans):
        at, high = slice(start, stop), slice(split + start, split + stop)
        start_copy(odd, q_ref.at[:, high], k_ref.at[:, at], a_buf.at[:, at], sems.at[0, i])
        start_copy(odd, o_ref.at[:, high], v_ref.at[:, at], b_buf.at[:, at], sems.at[1, i])
    tap_copy.start()
    for i, (start, stop, _) in enumerate(spans):
        at = slice(start, stop)
        pltpu.make_async_copy(k_ref.at[:, at], a_buf.at[:, at], sems.at[0, i]).wait()
        pltpu.make_async_copy(v_ref.at[:, at], b_buf.at[:, at], sems.at[1, i]).wait()
        pair_ref[:, at] = product(a_buf[:, at], b_buf[:, at])
    tap_copy.wait()
    quarter_ref[0] = tap_buf[...].astype(quarter_ref.dtype)


def cross_kernel(q_ref, k_ref, v_ref, o_ref, cross_ref):
    split = cross_ref.shape[1]
    for start, stop, _ in tiles(split, 1):
        low, high = slice(start, stop), slice(split + start, split + stop)

        @pl.when(my_parity() != 0)
        def _():
            cross_ref[:, low] = product(k_ref[:, low], v_ref[:, low])

        @pl.when(my_parity() == 0)
        def _():
            cross_ref[:, low] = product(q_ref[:, high], o_ref[:, high])


def late_kernel(q_ref, k_ref, v_ref, o_ref, docs_ref, masks_ref, pair_ref, cross_ref):
    split = cross_ref.shape[1]
    for start, stop, _ in tiles(split, 1):
        low, high = slice(start, stop), slice(split + start, split + stop)
        store_when(my_parity(), product(k_ref[:, high], v_ref[:, high]), cross_ref, pair_ref, low)
        store_when(my_parity(), product(q_ref[:, low], o_ref[:, low]), pair_ref, cross_ref, low)
    count, rows = docs_ref.shape
    index = lax.axis_index(BOTH)
    own = docs_ref[pl.ds(index, 1), :]
    before = docs_ref[pl.ds(jnp.maximum(index - 1, 0), 1), :]
    after = docs_ref[pl.ds(jnp.minimum(index + 1, count - 1), 1), :]
    first = own == own[:, 0:1]
    last = own == own[:, rows - 1 : rows]
    before = (before == own[:, 0:1]) & (index > 0)
    after = (after == own[:, rows - 1 : rows]) & (index < count - 1)
    lines = [jnp.where(line, 1.0, 0.0) for line in (first, ~first, before, after, last, last, last, last)]
    masks_ref[...] = jnp.concatenate(lines, 0).T


def store_when(flag, value, one_ref, other_ref, at):
    @pl.when(flag != 0)
    def _():
        one_ref[:, at] = value

    @pl.when(flag == 0)
    def _():
        other_ref[:, at] = value


def spectra_kernel(
    q_ref, k_ref, v_ref, o_ref, masks_ref, fwd_ref, inv_ref, lags_ref, xa_ref, xb_ref, ga_ref, gb_ref
):
    first, rest = masks_ref[:, 0:1], masks_ref[:, 1:2]
    fwd = fwd_ref[...]
    for start, stop, _ in tiles(lags_ref.shape[1], 1):
        at = slice(start, stop)
        x, g = product(k_ref[:, at], v_ref[:, at]), product(q_ref[:, at], o_ref[:, at])
        xa, ga = dot(fwd, doubled(masked(x, first))), dot(fwd, doubled(masked(g, first)))
        xb, gb = dot(fwd, doubled(masked(x, rest))), dot(fwd, doubled(masked(g, rest)))
        xa_ref[:, at], ga_ref[:, at] = xa, ga
        xb_ref[:, at], gb_ref[:, at] = xb, gb
        lags_ref[:, at] = invert(inv_ref[...], times_conj(ga, xa) + times_conj(gb, xb))


def halo_of(low_if_odd, low_if_even, start, stop):
    split = low_if_odd.shape[1]
    at = slice(start % split, start % split + stop - start)
    one, two = (low_if_odd, low_if_even) if start < split else (low_if_even, low_if_odd)
    return pick(my_parity(), one[:, at], two[:, at])


def lags_kernel(
    pair_ref, cross_ref, own_ref, xa_ref, xb_ref, ga_ref, masks_ref,
    prior_fwd_ref, next_fwd_ref, inv_ref, keep_ref, halo_ref, *sends,
):
    rows = masks_ref.shape[0]
    before, after = masks_ref[:, 2:3], masks_ref[:, 3:4]
    single = masks_ref[rows - 1 : rows, 0:1] > 0.0
    chans, half = keep_ref.shape[2], keep_ref.shape[1]
    me, core = my_ctx(), my_core()
    split = pair_ref.shape[1]
    spans = tiles(2 * split, chans)
    for start, stop, groups in spans:
        at = slice(start, stop)
        halo = halo_of(pair_ref, cross_ref, start, stop)
        halo_ref[:, at] = halo
        if start < split:
            prior = dot(prior_fwd_ref[...], doubled(masked(halo, before)))
            spectrum = times_conj(ga_ref[:, at], prior)
        else:
            later = dot(next_fwd_ref[...], doubled(masked(halo, after)))
            spectrum = times_conj(later, jnp.where(single, xa_ref[:, at], xb_ref[:, at]))
        lags = own_ref[:, at] + invert(inv_ref[...], spectrum)
        low, high = lags[:half], lags[half:]
        keep, send = pick(core, high, low), pick(core, low, high)
        for j, group in enumerate(groups):
            keep_ref[group ^ me] = keep[:, j * chans : (j + 1) * chans]
            place, value = group ^ me, send[:, j * chans : (j + 1) * chans].astype(BF16)
            for near, send_ref in enumerate(sends):

                @pl.when(place // 2 == near)
                def _(send_ref=send_ref):
                    send_ref[place % 2] = value


def middle_kernel(
    halo_ref, k_ref, v_ref, o_ref, xa_ref, xb_ref, ga_ref, gb_ref, near_ref, far_ref, other_near_ref, other_far_ref,
    masks_ref, fwd_ref, prior_fwd_ref, next_fwd_ref, inv_ref,
    taps_ref, mixed_ref, back_ref, q_out, k_out, v_out,
):
    first, rest, before, after, last = (masks_ref[:, i : i + 1] for i in range(5))
    inv_two = masked_inverse(inv_ref[...], first, rest)
    inv_three = masked_inverse(inv_ref[...], first, rest, last)
    me, quarter = my_ctx(), my_quarter()
    split = q_out.shape[1]
    shares = (near_ref, far_ref), (other_near_ref, other_far_ref)
    chans = 4 * near_ref.shape[1]
    for start, stop, groups in tiles(2 * split, chans):
        parts = []
        for group in groups:
            for r in range(4):
                place = r ^ quarter
                mine, other = (pick(place // 2, far[group ^ me], near[group ^ me]) for near, far in shares)
                parts.append(pick(place % 2, other, mine))
        at = slice(start, stop)
        taps = tap_spectrum(fwd_ref[...], jnp.concatenate(parts, 0))
        taps_ref[:, at] = taps
        halo = halo_ref[:, at]
        xa, xb, ga, gb = (ref[:, at] for ref in (xa_ref, xb_ref, ga_ref, gb_ref))
        if start < split:
            prior = dot(prior_fwd_ref[...], doubled(masked(halo, before)))
            mixed = invert(inv_two, times(xa + prior, taps), times(xb, taps))
            q_out[:, at] = (o_ref[:, at].astype(F32) * mixed).astype(q_out.dtype)
            back_ref[:, at] = invert(inv_two, times_conj(ga, taps), times_conj(gb, taps))
        else:
            mine = slice(start - split, stop - split)
            later = dot(next_fwd_ref[...], doubled(masked(halo, after)))
            mixed_ref[:, mine] = invert(inv_two, times(xa, taps), times(xb, taps))
            back = invert(inv_three, times_conj(ga, taps), times_conj(gb, taps), times_conj(later, taps))
            k_out[:, mine] = (back * v_ref[:, at].astype(F32)).astype(k_out.dtype)
            v_out[:, mine] = (back * k_ref[:, at].astype(F32)).astype(v_out.dtype)


def last_kernel(
    pair_ref, cross_ref, k_ref, v_ref, o_ref, taps_ref, mixed_ref, back_ref, q_half, k_half, v_half,
    masks_ref, prior_fwd_ref, next_fwd_ref, inv_ref, q_out, k_out, v_out, mark_ref,
    q_buf, k_buf, v_buf, out_sems,
):
    mark_ref[...] = jnp.zeros_like(mark_ref)
    first, before, after, last = (masks_ref[:, i : i + 1] for i in (0, 2, 3, 4))
    inv_first = masked_inverse(inv_ref[...], first)
    inv_last = masked_inverse(inv_ref[...], last)
    split = pair_ref.shape[1]
    spans = tiles(2 * split, 1)
    copies = []

    def send(source, target):
        copies.append(pltpu.make_async_copy(source, target, out_sems.at[len(copies)]))
        copies[-1].start()

    send(q_half, q_out.at[:, :split])
    send(k_half, k_out.at[:, split:])
    send(v_half, v_out.at[:, split:])
    for start, stop, _ in spans:
        at = slice(start, stop)
        taps = taps_ref[:, at]
        halo = halo_of(cross_ref, pair_ref, start, stop)
        if start < split:
            later = dot(next_fwd_ref[...], doubled(masked(halo, after)))
            back = back_ref[:, at] + invert(inv_last, times_conj(later, taps))
            k_buf[:, at] = (back * v_ref[:, at].astype(F32)).astype(k_buf.dtype)
            v_buf[:, at] = (back * k_ref[:, at].astype(F32)).astype(v_buf.dtype)
            send(k_buf.at[:, at], k_out.at[:, at])
            send(v_buf.at[:, at], v_out.at[:, at])
        else:
            mine = slice(start - split, stop - split)
            prior = dot(prior_fwd_ref[...], doubled(masked(halo, before)))
            mixed = mixed_ref[:, mine] + invert(inv_first, times(prior, taps))
            q_buf[:, mine] = (o_ref[:, at].astype(F32) * mixed).astype(q_buf.dtype)
            send(q_buf.at[:, mine], q_out.at[:, at])
    for copy in copies:
        copy.wait()


def first_sum_kernel(count, keep_ref, *refs):
    for j, (swapped_ref, out_ref) in enumerate(zip(refs[:count], refs[count:])):
        out_ref[...] = (keep_ref[2 * j : 2 * j + 2] + swapped_ref[...].astype(F32)).astype(out_ref.dtype)


def second_sum_kernel(count, *refs):
    total = refs[0][...]
    for ref in refs[1:count]:
        total = total + ref[...].astype(F32)
    own_ref, low_ref, high_ref = refs[count:]
    own_ref[...] = total[0]
    low_ref[...] = total[0].astype(low_ref.dtype)
    high_ref[...] = total[1].astype(high_ref.dtype)


def third_sum_kernel(count, *refs):
    total = refs[0][...]
    for ref in refs[1:count]:
        total = total + ref[...].astype(F32)
    for ref in refs[count:]:
        ref[...] = total


def finish_kernel(scale, mine_ref, other_ref, out_ref):
    mine, other = mine_ref[...], other_ref[...]
    core = my_core()
    low = jnp.where(core == 0, mine, other)
    high = jnp.where(core == 0, other, mine)
    out_ref[...] = jnp.concatenate([low, high], 0).T * scale


def swap(value, axis, bit):
    count = lax.axis_size(axis)
    return lax.ppermute(value, axis, [(i, i ^ bit) for i in range(count)])


def cross(value, dp_bits, ctx_bits):
    dp, ctx = lax.axis_size("dp"), lax.axis_size("ctx")
    pairs = [(d * ctx + c, (d ^ dp_bits) * ctx + (c ^ ctx_bits)) for d in range(dp) for c in range(ctx)]
    return lax.ppermute(value, BOTH, pairs)


def bits_of(count):
    assert count & (count - 1) == 0
    return [1 << b for b in range(count.bit_length() - 1)]


def gather_near_taps(mine):
    pair = jnp.concatenate([mine, swap(mine, "ctx", 1)], 0)
    return jnp.concatenate([pair] + [swap(pair, "ctx", j) for j in range(2, lax.axis_size("ctx"), 2)], 0)


def gather_far_taps(near):
    far = swap(near, "dp", 2)
    return near, far, swap(near, "dp", 1), swap(far, "dp", 1)


def shards(query_act, key_act, value_act, out_grad, filter_taps, doc_ids):
    rows, width = query_act.shape
    chans, tap_count = filter_taps.shape
    dp, ctx = lax.axis_size("dp"), lax.axis_size("ctx")
    assert rows == tap_count and chans * ctx == width
    scale = 1.0 / math.sqrt(doc_ids.shape[0])
    count = dp * ctx
    fwd, prior_fwd, next_fwd, (inv_high, inv_low) = transforms(tap_count)
    inv = np.concatenate([inv_high, inv_low], 0)
    fwd, prior_fwd, next_fwd, inv = map(jnp.asarray, (fwd, prior_fwd, next_fwd, inv))

    split = width // 2
    pairs = [(i, i ^ 1) for i in range(count)]
    crosses = [(i, i + 1 if i % 2 else i - 1) for i in range(1, count - 1)]
    vmem = pl.BlockSpec(memory_space=pltpu.VMEM)
    anywhere = pl.BlockSpec(memory_space=pl.ANY)
    hbm = pl.BlockSpec(memory_space=pltpu.HBM)
    streamed = pl.BlockSpec()

    def call(kernel, outs, *args, after=(), direct=0, out_specs=None, scratch=(), limit=8, flops=1):
        read = len(args)
        return pl.pallas_call(
            lambda *refs: kernel(*refs[:read], *refs[read + len(after) :]),
            out_shape=outs,
            in_specs=[hbm] * direct + [vmem] * (read - direct) + [anywhere] * len(after),
            out_specs=jax.tree.map(lambda _: vmem, outs) if out_specs is None else out_specs,
            scratch_shapes=scratch,
            compiler_params=pltpu.CompilerParams(vmem_limit_bytes=limit * 1024 * 1024),
            cost_estimate=pl.CostEstimate(flops=flops, bytes_accessed=1, transcendentals=0),
        )(*args, *after)

    sds = jax.ShapeDtypeStruct
    act = sds((rows, width), BF16)
    full = sds((2 * rows, width), F32)
    half_act = sds((rows, split), BF16)
    half_sum = sds((rows, split), F32)
    n_tiles = len(tiles(width, chans))

    share = chans // 4
    acts = (query_act, key_act, value_act, out_grad)
    sent, taps_quarter = call(
        prelude_kernel,
        (half_act, sds((1, share, tap_count), BF16)),
        *acts, filter_taps,
        direct=5, out_specs=(vmem, vmem),
        scratch=[
            pltpu.VMEM((rows, split), BF16),
            pltpu.VMEM((rows, split), BF16),
            pltpu.VMEM((share, tap_count), F32),
            pltpu.SemaphoreType.DMA((2, n_tiles)),
            pltpu.SemaphoreType.DMA,
        ],
        limit=56,
    )
    pair_early = lax.ppermute(sent, BOTH, pairs)
    taps_near = gather_near_taps(taps_quarter)
    sent = call(cross_kernel, half_act, *acts, after=(taps_near, pair_early), out_specs=streamed)
    cross_early = lax.ppermute(sent, BOTH, crosses)
    masks, pair_sent, cross_sent = call(
        late_kernel,
        (sds((rows, 8), F32), half_act, half_act),
        *acts, doc_ids.reshape(-1, rows),
        after=(sent,), out_specs=(vmem, streamed, streamed),
    )
    cross_late = lax.ppermute(cross_sent, BOTH, crosses)
    pair_late = lax.ppermute(pair_sent, BOTH, pairs)
    taps_all = gather_far_taps(taps_near)
    own_lags, xa, xb, ga, gb = call(
        spectra_kernel,
        (sds((rows, width), F32), full, full, full, full),
        *acts, masks, fwd, inv,
        limit=16,
    )
    pair = (2, rows // 2, chans)
    keep, halo, *sends = call(
        lags_kernel,
        (sds((ctx, rows // 2, chans), F32), act) + (sds(pair, BF16),) * (ctx // 2),
        pair_early, cross_early, own_lags, xa, xb, ga, masks, prior_fwd, next_fwd, inv,
        out_specs=(vmem, vmem) + (streamed,) * (ctx // 2), limit=12,
    )
    spectrum, own_mixed, own_back, query_half, key_half, value_half = call(
        middle_kernel,
        (full, half_sum, half_sum, half_act, half_act, half_act),
        halo, key_act, value_act, out_grad, xa, xb, ga, gb, *taps_all,
        masks, fwd, prior_fwd, next_fwd, inv,
        after=(sends[0], cross_late), limit=16,
    )

    near = [j for j in range(2, ctx, 2)]
    own, *sends = call(
        functools.partial(first_sum_kernel, ctx // 2),
        (sds(pair, F32),) + (sds(pair, BF16),) * len(near),
        keep, *(swap(value, "dp", 1) for value in sends),
        out_specs=(vmem,) + (streamed,) * len(near),
    )
    routes = list(zip(sends, near))
    got = [swap(value, "ctx", j) for value, j in routes[1:] + routes[:1]]
    query_grad, key_grad, value_grad, mark = call(
        last_kernel,
        (act, act, act, sds((8, 128), F32)),
        pair_late, cross_late, key_act, value_act, out_grad, spectrum, own_mixed, own_back,
        query_half, key_half, value_half, masks, prior_fwd, next_fwd, inv,
        out_specs=(hbm, hbm, hbm, vmem), limit=14,
        scratch=[pltpu.VMEM((rows, split), BF16)] * 3 + [pltpu.SemaphoreType.DMA((3 + 2 * n_tiles,))],
    )
    piece = pair[1:]
    own, low, high = call(
        functools.partial(second_sum_kernel, 1 + len(got)),
        (sds(piece, F32), sds(piece, BF16), sds(piece, BF16)),
        own, *got,
        after=(query_half,), out_specs=(vmem, streamed, streamed),
    )
    got = [
        cross(high if j else low, d, j) for d in reversed(range(0, dp, 2)) for j in (1, 0) if d or j
    ]
    total, total_sent = call(
        functools.partial(third_sum_kernel, 1 + len(got)),
        (sds(piece, F32), sds(piece, F32)),
        own, *got,
        after=(mark,), out_specs=(vmem, streamed),
    )
    filter_grad = call(
        functools.partial(finish_kernel, scale), sds((chans, tap_count), F32), total, swap(total_sent, "dp", 1),
    )
    return (query_grad, key_grad, value_grad, filter_grad)


def solution(mesh):
    in_specs = (
        P(BOTH, None),
        P(BOTH, None),
        P(BOTH, None),
        P(BOTH, None),
        P("ctx", None),
        P(),
    )
    out_specs = (
        P(BOTH, None),
        P(BOTH, None),
        P(BOTH, None),
        P("ctx", None),
    )
    return jax.shard_map(shards, mesh=mesh, in_specs=in_specs, out_specs=out_specs, check_vma=False)
```

```python
import functools
import math

import jax
import jax.numpy as jnp
import ml_dtypes
import numpy as np
from jax import lax
from jax.experimental import pallas as pl
from jax.experimental.pallas import tpu as pltpu
from jax.sharding import PartitionSpec as P

BOTH = ("dp", "ctx")
F32 = jnp.float32
BF16 = jnp.bfloat16


def split_bf16(matrix):
    high = matrix.astype(ml_dtypes.bfloat16)
    low = (matrix - high.astype(np.float64)).astype(ml_dtypes.bfloat16)
    return high, low


def transforms(count):
    freq = np.arange(count) + 0.5
    place = np.arange(count)

    def forward(offset):
        angle = np.pi / count * np.outer(freq, place + offset)
        high, low = split_bf16(np.concatenate([np.cos(angle), -np.sin(angle)], 0))
        return np.concatenate([high, low], 1)

    angle = np.pi / count * np.outer(place, freq)
    inverse = np.concatenate([np.cos(angle), -np.sin(angle)], 1) / count
    return forward(0), forward(-count), forward(count), split_bf16(inverse)


def dot(a, b):
    return jnp.dot(a, b, preferred_element_type=F32)


def doubled(block):
    return jnp.concatenate([block, block], 0)


def tap_spectrum(fwd, taps):
    both = jnp.concatenate([taps, taps], 1)
    return lax.dot_general(fwd, both, (((1,), (1,)), ((), ())), preferred_element_type=F32)


def halves(spectrum):
    count = spectrum.shape[0] // 2
    return spectrum[:count], spectrum[count:]


def times(a, b):
    ar, ai = halves(a)
    br, bi = halves(b)
    return jnp.concatenate([ar * br - ai * bi, ar * bi + ai * br], 0)


def times_conj(a, b):
    ar, ai = halves(a)
    br, bi = halves(b)
    return jnp.concatenate([ar * br + ai * bi, ai * br - ar * bi], 0)


def invert(inv, *spectra):
    out = dot(inv, jnp.concatenate([spectrum.astype(BF16) for spectrum in spectra], 0))
    count = out.shape[0] // 2
    return out[:count] + out[count:]


def masked(block, mask):
    return block * mask.astype(BF16)


def masked_inverse(inv, *masks):
    return jnp.concatenate([masked(inv, doubled(mask)) for mask in masks], 1)


def tiles(width, chans):
    tile = max(chans, 1024)
    spans = [(start, min(start + tile, width)) for start in range(0, width, tile)]
    return [(start, stop, range(start // chans, stop // chans)) for start, stop in spans]


def pick(flag, one, other):
    return jnp.where(flag != 0, one, other)


def product(a, b):
    return (a.astype(F32) * b.astype(F32)).astype(BF16)


def my_ctx():
    return lax.axis_index("ctx")


def my_quarter():
    return lax.axis_index("dp") % 4


def my_core():
    return lax.axis_index("dp") % 2


def my_parity():
    return lax.axis_index("ctx") % 2


def start_copy(flag, one, other, target, sem):
    @pl.when(flag != 0)
    def _():
        pltpu.make_async_copy(one, target, sem).start()

    @pl.when(flag == 0)
    def _():
        pltpu.make_async_copy(other, target, sem).start()


def prelude_kernel(
    q_ref, k_ref, v_ref, o_ref, taps_ref, pair_ref, quarter_ref, a_buf, b_buf, tap_buf, sems, tap_sem
):
    split = pair_ref.shape[1]
    share = tap_buf.shape[0]
    rows = pl.ds(pl.multiple_of(my_quarter() * share, share), share)
    tap_copy = pltpu.make_async_copy(taps_ref.at[rows, :], tap_buf, tap_sem)
    spans = tiles(split, 1)
    odd = my_parity()
    for i, (start, stop, _) in enumerate(spans):
        at, high = slice(start, stop), slice(split + start, split + stop)
        start_copy(odd, q_ref.at[:, high], k_ref.at[:, at], a_buf.at[:, at], sems.at[0, i])
        start_copy(odd, o_ref.at[:, high], v_ref.at[:, at], b_buf.at[:, at], sems.at[1, i])
    tap_copy.start()
    for i, (start, stop, _) in enumerate(spans):
        at = slice(start, stop)
        pltpu.make_async_copy(k_ref.at[:, at], a_buf.at[:, at], sems.at[0, i]).wait()
        pltpu.make_async_copy(v_ref.at[:, at], b_buf.at[:, at], sems.at[1, i]).wait()
        pair_ref[:, at] = product(a_buf[:, at], b_buf[:, at])
    tap_copy.wait()
    quarter_ref[0] = tap_buf[...].astype(quarter_ref.dtype)


def cross_kernel(q_ref, k_ref, v_ref, o_ref, cross_ref):
    split = cross_ref.shape[1]
    for start, stop, _ in tiles(split, 1):
        low, high = slice(start, stop), slice(split + start, split + stop)

        @pl.when(my_parity() != 0)
        def _():
            cross_ref[:, low] = product(k_ref[:, low], v_ref[:, low])

        @pl.when(my_parity() == 0)
        def _():
            cross_ref[:, low] = product(q_ref[:, high], o_ref[:, high])


def late_kernel(q_ref, k_ref, v_ref, o_ref, docs_ref, masks_ref, pair_ref, cross_ref):
    split = cross_ref.shape[1]
    for start, stop, _ in tiles(split, 1):
        low, high = slice(start, stop), slice(split + start, split + stop)
        store_when(my_parity(), product(k_ref[:, high], v_ref[:, high]), cross_ref, pair_ref, low)
        store_when(my_parity(), product(q_ref[:, low], o_ref[:, low]), pair_ref, cross_ref, low)
    count, rows = docs_ref.shape
    index = lax.axis_index(BOTH)
    own = docs_ref[pl.ds(index, 1), :]
    before = docs_ref[pl.ds(jnp.maximum(index - 1, 0), 1), :]
    after = docs_ref[pl.ds(jnp.minimum(index + 1, count - 1), 1), :]
    first = own == own[:, 0:1]
    last = own == own[:, rows - 1 : rows]
    before = (before == own[:, 0:1]) & (index > 0)
    after = (after == own[:, rows - 1 : rows]) & (index < count - 1)
    lines = [jnp.where(line, 1.0, 0.0) for line in (first, ~first, before, after, last, last, last, last)]
    masks_ref[...] = jnp.concatenate(lines, 0).T


def store_when(flag, value, one_ref, other_ref, at):
    @pl.when(flag != 0)
    def _():
        one_ref[:, at] = value

    @pl.when(flag == 0)
    def _():
        other_ref[:, at] = value


def spectra_kernel(
    q_ref, k_ref, v_ref, o_ref, masks_ref, fwd_ref, inv_ref, lags_ref, xa_ref, xb_ref, ga_ref, gb_ref
):
    first, rest = masks_ref[:, 0:1], masks_ref[:, 1:2]
    fwd = fwd_ref[...]
    for start, stop, _ in tiles(lags_ref.shape[1], 1):
        at = slice(start, stop)
        x, g = product(k_ref[:, at], v_ref[:, at]), product(q_ref[:, at], o_ref[:, at])
        xa, ga = dot(fwd, doubled(masked(x, first))), dot(fwd, doubled(masked(g, first)))
        xb, gb = dot(fwd, doubled(masked(x, rest))), dot(fwd, doubled(masked(g, rest)))
        xa_ref[:, at], ga_ref[:, at] = xa, ga
        xb_ref[:, at], gb_ref[:, at] = xb, gb
        lags_ref[:, at] = invert(inv_ref[...], times_conj(ga, xa) + times_conj(gb, xb))


def halo_of(low_if_odd, low_if_even, start, stop):
    split = low_if_odd.shape[1]
    at = slice(start % split, start % split + stop - start)
    one, two = (low_if_odd, low_if_even) if start < split else (low_if_even, low_if_odd)
    return pick(my_parity(), one[:, at], two[:, at])


def lags_kernel(
    pair_ref, cross_ref, own_ref, xa_ref, xb_ref, ga_ref, masks_ref,
    prior_fwd_ref, next_fwd_ref, inv_ref, keep_ref, halo_ref, *sends,
):
    rows = masks_ref.shape[0]
    before, after = masks_ref[:, 2:3], masks_ref[:, 3:4]
    single = masks_ref[rows - 1 : rows, 0:1] > 0.0
    chans, half = keep_ref.shape[2], keep_ref.shape[1]
    me, core = my_ctx(), my_core()
    split = pair_ref.shape[1]
    spans = tiles(2 * split, chans)
    for start, stop, groups in spans:
        at = slice(start, stop)
        halo = halo_of(pair_ref, cross_ref, start, stop)
        halo_ref[:, at] = halo
        if start < split:
            prior = dot(prior_fwd_ref[...], doubled(masked(halo, before)))
            spectrum = times_conj(ga_ref[:, at], prior)
        else:
            later = dot(next_fwd_ref[...], doubled(masked(halo, after)))
            spectrum = times_conj(later, jnp.where(single, xa_ref[:, at], xb_ref[:, at]))
        lags = own_ref[:, at] + invert(inv_ref[...], spectrum)
        low, high = lags[:half], lags[half:]
        keep, send = pick(core, high, low), pick(core, low, high)
        for j, group in enumerate(groups):
            keep_ref[group ^ me] = keep[:, j * chans : (j + 1) * chans]
            place, value = group ^ me, send[:, j * chans : (j + 1) * chans].astype(BF16)
            for near, send_ref in enumerate(sends):

                @pl.when(place // 2 == near)
                def _(send_ref=send_ref):
                    send_ref[place % 2] = value


def middle_kernel(
    halo_ref, k_ref, v_ref, o_ref, xa_ref, xb_ref, ga_ref, gb_ref, near_ref, far_ref, other_near_ref, other_far_ref,
    masks_ref, fwd_ref, prior_fwd_ref, next_fwd_ref, inv_ref,
    taps_ref, mixed_ref, back_ref, q_out, k_out, v_out,
):
    first, rest, before, after, last = (masks_ref[:, i : i + 1] for i in range(5))
    inv_two = masked_inverse(inv_ref[...], first, rest)
    inv_three = masked_inverse(inv_ref[...], first, rest, last)
    me, quarter = my_ctx(), my_quarter()
    split = q_out.shape[1]
    shares = (near_ref, far_ref), (other_near_ref, other_far_ref)
    chans = 4 * near_ref.shape[1]
    for start, stop, groups in tiles(2 * split, chans):
        parts = []
        for group in groups:
            for r in range(4):
                place = r ^ quarter
                mine, other = (pick(place // 2, far[group ^ me], near[group ^ me]) for near, far in shares)
                parts.append(pick(place % 2, other, mine))
        at = slice(start, stop)
        taps = tap_spectrum(fwd_ref[...], jnp.concatenate(parts, 0))
        taps_ref[:, at] = taps
        halo = halo_ref[:, at]
        xa, xb, ga, gb = (ref[:, at] for ref in (xa_ref, xb_ref, ga_ref, gb_ref))
        if start < split:
            prior = dot(prior_fwd_ref[...], doubled(masked(halo, before)))
            mixed = invert(inv_two, times(xa + prior, taps), times(xb, taps))
            q_out[:, at] = (o_ref[:, at].astype(F32) * mixed).astype(q_out.dtype)
            back_ref[:, at] = invert(inv_two, times_conj(ga, taps), times_conj(gb, taps))
        else:
            mine = slice(start - split, stop - split)
            later = dot(next_fwd_ref[...], doubled(masked(halo, after)))
            mixed_ref[:, mine] = invert(inv_two, times(xa, taps), times(xb, taps))
            back = invert(inv_three, times_conj(ga, taps), times_conj(gb, taps), times_conj(later, taps))
            k_out[:, mine] = (back * v_ref[:, at].astype(F32)).astype(k_out.dtype)
            v_out[:, mine] = (back * k_ref[:, at].astype(F32)).astype(v_out.dtype)


def last_kernel(
    pair_ref, cross_ref, k_ref, v_ref, o_ref, taps_ref, mixed_ref, back_ref, q_half, k_half, v_half,
    masks_ref, prior_fwd_ref, next_fwd_ref, inv_ref, q_out, k_out, v_out, mark_ref,
    q_buf, k_buf, v_buf, out_sems,
):
    mark_ref[...] = jnp.zeros_like(mark_ref)
    first, before, after, last = (masks_ref[:, i : i + 1] for i in (0, 2, 3, 4))
    inv_first = masked_inverse(inv_ref[...], first)
    inv_last = masked_inverse(inv_ref[...], last)
    split = pair_ref.shape[1]
    spans = tiles(2 * split, 1)
    copies = []

    def send(source, target):
        copies.append(pltpu.make_async_copy(source, target, out_sems.at[len(copies)]))
        copies[-1].start()

    send(q_half, q_out.at[:, :split])
    send(k_half, k_out.at[:, split:])
    send(v_half, v_out.at[:, split:])
    for start, stop, _ in spans:
        at = slice(start, stop)
        taps = taps_ref[:, at]
        halo = halo_of(cross_ref, pair_ref, start, stop)
        if start < split:
            later = dot(next_fwd_ref[...], doubled(masked(halo, after)))
            back = back_ref[:, at] + invert(inv_last, times_conj(later, taps))
            k_buf[:, at] = (back * v_ref[:, at].astype(F32)).astype(k_buf.dtype)
            v_buf[:, at] = (back * k_ref[:, at].astype(F32)).astype(v_buf.dtype)
            send(k_buf.at[:, at], k_out.at[:, at])
            send(v_buf.at[:, at], v_out.at[:, at])
        else:
            mine = slice(start - split, stop - split)
            prior = dot(prior_fwd_ref[...], doubled(masked(halo, before)))
            mixed = mixed_ref[:, mine] + invert(inv_first, times(prior, taps))
            q_buf[:, mine] = (o_ref[:, at].astype(F32) * mixed).astype(q_buf.dtype)
            send(q_buf.at[:, mine], q_out.at[:, at])
    for copy in copies:
        copy.wait()


def first_sum_kernel(count, keep_ref, *refs):
    for j, (swapped_ref, out_ref) in enumerate(zip(refs[:count], refs[count:])):
        out_ref[...] = (keep_ref[2 * j : 2 * j + 2] + swapped_ref[...].astype(F32)).astype(out_ref.dtype)


def second_sum_kernel(count, *refs):
    total = refs[0][...]
    for ref in refs[1:count]:
        total = total + ref[...].astype(F32)
    own_ref, low_ref, high_ref = refs[count:]
    own_ref[...] = total[0]
    low_ref[...] = total[0].astype(low_ref.dtype)
    high_ref[...] = total[1].astype(high_ref.dtype)


def third_sum_kernel(count, *refs):
    total = refs[0][...]
    for ref in refs[1:count]:
        total = total + ref[...].astype(F32)
    for ref in refs[count:]:
        ref[...] = total


def finish_kernel(scale, mine_ref, other_ref, out_ref):
    mine, other = mine_ref[...], other_ref[...]
    core = my_core()
    low = jnp.where(core == 0, mine, other)
    high = jnp.where(core == 0, other, mine)
    out_ref[...] = jnp.concatenate([low, high], 0).T * scale


def swap(value, axis, bit):
    count = lax.axis_size(axis)
    return lax.ppermute(value, axis, [(i, i ^ bit) for i in range(count)])


def cross(value, dp_bits, ctx_bits):
    dp, ctx = lax.axis_size("dp"), lax.axis_size("ctx")
    pairs = [(d * ctx + c, (d ^ dp_bits) * ctx + (c ^ ctx_bits)) for d in range(dp) for c in range(ctx)]
    return lax.ppermute(value, BOTH, pairs)


def bits_of(count):
    assert count & (count - 1) == 0
    return [1 << b for b in range(count.bit_length() - 1)]


def gather_near_taps(mine):
    pair = jnp.concatenate([mine, swap(mine, "ctx", 1)], 0)
    return jnp.concatenate([pair] + [swap(pair, "ctx", j) for j in range(2, lax.axis_size("ctx"), 2)], 0)


def gather_far_taps(near):
    far = swap(near, "dp", 2)
    return near, far, swap(near, "dp", 1), swap(far, "dp", 1)


def shards(query_act, key_act, value_act, out_grad, filter_taps, doc_ids):
    rows, width = query_act.shape
    chans, tap_count = filter_taps.shape
    dp, ctx = lax.axis_size("dp"), lax.axis_size("ctx")
    assert rows == tap_count and chans * ctx == width
    scale = 1.0 / math.sqrt(doc_ids.shape[0])
    count = dp * ctx
    fwd, prior_fwd, next_fwd, (inv_high, inv_low) = transforms(tap_count)
    inv = np.concatenate([inv_high, inv_low], 0)
    fwd, prior_fwd, next_fwd, inv = map(jnp.asarray, (fwd, prior_fwd, next_fwd, inv))

    split = width // 2
    pairs = [(i, i ^ 1) for i in range(count)]
    crosses = [(i, i + 1 if i % 2 else i - 1) for i in range(1, count - 1)]
    vmem = pl.BlockSpec(memory_space=pltpu.VMEM)
    anywhere = pl.BlockSpec(memory_space=pl.ANY)
    hbm = pl.BlockSpec(memory_space=pltpu.HBM)
    streamed = pl.BlockSpec()

    def call(kernel, outs, *args, after=(), direct=0, out_specs=None, scratch=(), limit=8, flops=1):
        read = len(args)
        return pl.pallas_call(
            lambda *refs: kernel(*refs[:read], *refs[read + len(after) :]),
            out_shape=outs,
            in_specs=[hbm] * direct + [vmem] * (read - direct) + [anywhere] * len(after),
            out_specs=jax.tree.map(lambda _: vmem, outs) if out_specs is None else out_specs,
            scratch_shapes=scratch,
            compiler_params=pltpu.CompilerParams(vmem_limit_bytes=limit * 1024 * 1024),
            cost_estimate=pl.CostEstimate(flops=flops, bytes_accessed=1, transcendentals=0),
        )(*args, *after)

    sds = jax.ShapeDtypeStruct
    act = sds((rows, width), BF16)
    full = sds((2 * rows, width), F32)
    half_act = sds((rows, split), BF16)
    half_sum = sds((rows, split), F32)
    n_tiles = len(tiles(width, chans))

    share = chans // 4
    acts = (query_act, key_act, value_act, out_grad)
    sent, taps_quarter = call(
        prelude_kernel,
        (half_act, sds((1, share, tap_count), BF16)),
        *acts, filter_taps,
        direct=5, out_specs=(vmem, vmem),
        scratch=[
            pltpu.VMEM((rows, split), BF16),
            pltpu.VMEM((rows, split), BF16),
            pltpu.VMEM((share, tap_count), F32),
            pltpu.SemaphoreType.DMA((2, n_tiles)),
            pltpu.SemaphoreType.DMA,
        ],
        limit=56,
    )
    pair_early = lax.ppermute(sent, BOTH, pairs)
    taps_near = gather_near_taps(taps_quarter)
    sent = call(cross_kernel, half_act, *acts, after=(taps_near, pair_early), out_specs=streamed)
    cross_early = lax.ppermute(sent, BOTH, crosses)
    masks, pair_sent, cross_sent = call(
        late_kernel,
        (sds((rows, 8), F32), half_act, half_act),
        *acts, doc_ids.reshape(-1, rows),
        after=(sent,), out_specs=(vmem, streamed, streamed),
    )
    cross_late = lax.ppermute(cross_sent, BOTH, crosses)
    pair_late = lax.ppermute(pair_sent, BOTH, pairs)
    taps_all = gather_far_taps(taps_near)
    own_lags, xa, xb, ga, gb = call(
        spectra_kernel,
        (sds((rows, width), F32), full, full, full, full),
        *acts, masks, fwd, inv,
        limit=16,
    )
    pair = (2, rows // 2, chans)
    keep, halo, *sends = call(
        lags_kernel,
        (sds((ctx, rows // 2, chans), F32), act) + (sds(pair, BF16),) * (ctx // 2),
        pair_early, cross_early, own_lags, xa, xb, ga, masks, prior_fwd, next_fwd, inv,
        out_specs=(vmem, vmem) + (streamed,) * (ctx // 2), limit=12,
    )
    spectrum, own_mixed, own_back, query_half, key_half, value_half = call(
        middle_kernel,
        (full, half_sum, half_sum, half_act, half_act, half_act),
        halo, key_act, value_act, out_grad, xa, xb, ga, gb, *taps_all,
        masks, fwd, prior_fwd, next_fwd, inv,
        after=(sends[0], cross_late), limit=16,
    )

    near = [j for j in range(2, ctx, 2)]
    own, *sends = call(
        functools.partial(first_sum_kernel, ctx // 2),
        (sds(pair, F32),) + (sds(pair, BF16),) * len(near),
        keep, *(swap(value, "dp", 1) for value in sends),
        out_specs=(vmem,) + (streamed,) * len(near),
    )
    routes = list(zip(sends, near))
    got = [swap(value, "ctx", j) for value, j in routes[1:] + routes[:1]]
    query_grad, key_grad, value_grad, mark = call(
        last_kernel,
        (act, act, act, sds((8, 128), F32)),
        pair_late, cross_late, key_act, value_act, out_grad, spectrum, own_mixed, own_back,
        query_half, key_half, value_half, masks, prior_fwd, next_fwd, inv,
        out_specs=(hbm, hbm, hbm, vmem), limit=14,
        scratch=[pltpu.VMEM((rows, split), BF16)] * 3 + [pltpu.SemaphoreType.DMA((3 + 2 * n_tiles,))],
    )
    piece = pair[1:]
    own, low, high = call(
        functools.partial(second_sum_kernel, 1 + len(got)),
        (sds(piece, F32), sds(piece, BF16), sds(piece, BF16)),
        own, *got,
        after=(query_half,), out_specs=(vmem, streamed, streamed),
    )
    got = [
        cross(high if j else low, d, j) for j in (1, 0) for d in reversed(range(0, dp, 2)) if d or j
    ]
    total, total_sent = call(
        functools.partial(third_sum_kernel, 1 + len(got)),
        (sds(piece, F32), sds(piece, F32)),
        own, *got,
        after=(mark,), out_specs=(vmem, streamed),
    )
    filter_grad = call(
        functools.partial(finish_kernel, scale), sds((chans, tap_count), F32), total, swap(total_sent, "dp", 1),
    )
    return (query_grad, key_grad, value_grad, filter_grad)


def solution(mesh):
    in_specs = (
        P(BOTH, None),
        P(BOTH, None),
        P(BOTH, None),
        P(BOTH, None),
        P("ctx", None),
        P(),
    )
    out_specs = (
        P(BOTH, None),
        P(BOTH, None),
        P(BOTH, None),
        P("ctx", None),
    )
    return jax.shard_map(shards, mesh=mesh, in_specs=in_specs, out_specs=out_specs, check_vma=False)
```
